32 devices in a mesh: dp: 2 (over y), row: 4 (over z), col: 4 (over x, core).
Axes of the slice: x: 2, y: 2, z: 4, core: 2. Of those that a mesh axis runs over, the one named last changes fastest.
Arguments:
- tokens: bfloat16 [4728, 768], P(('dp', 'row')), may hold values from -6 to 6
- attn_gain: float32 [768], replicated, may hold values from 0.5 to 1.5
- attn_shift: float32 [768], replicated, may hold values from -3 to 3
- query_weight: bfloat16 [768, 768], P('col', 'row'), may hold values from -0.21875 to 0.21875
- key_weight: bfloat16 [768, 768], P('col', 'row'), may hold values from -0.21875 to 0.21875
- value_weight: bfloat16 [768, 768], P('col', 'row'), may hold values from -0.21875 to 0.21875
- query_bias: float32 [768], P('row'), may hold values from -3 to 3
- value_bias: float32 [768], P('row'), may hold values from -3 to 3
- proj_weight: bfloat16 [768, 768], P('row', 'col'), may hold values from -0.625 to 0.625
- proj_bias: float32 [768], P('col'), may hold values from -3 to 3
- mlp_gain: float32 [768], replicated, may hold values from 0.5 to 1.5
- mlp_shift: float32 [768], replicated, may hold values from -3 to 3
- expand_weight: bfloat16 [768, 3072], P('col', 'row'), may hold values from -0.21875 to 0.21875
- expand_bias: float32 [3072], P('row'), may hold values from -3 to 3
- shrink_weight: bfloat16 [768, 3072], P('col', 'row'), may hold values from -0.109375 to 0.109375
- shrink_bias: float32 [768], P('col'), may hold values from -3 to 3
- cotangent: bfloat16 [4728, 768], P(('dp', 'row')), may hold values from -6 to 6
Outputs:
- output: bfloat16 [4728, 768], P(('dp', 'row'))
- grad_tokens: bfloat16 [4728, 768], P(('dp', 'row'))
- grad_attn_gain: float32 [768], replicated
- grad_attn_shift: float32 [768], replicated
- grad_query_weight: float32 [768, 768], P('col', 'row')
- grad_key_weight: float32 [768, 768], P('col', 'row')
- grad_value_weight: float32 [768, 768], P('col', 'row')
- grad_query_bias: float32 [768], P('row')
- grad_value_bias: float32 [768], P('row')
- grad_proj_weight: float32 [768, 768], P('row', 'col')
- grad_proj_bias: float32 [768], P('col')
- grad_mlp_gain: float32 [768], replicated
- grad_mlp_shift: float32 [768], replicated
- grad_expand_weight: float32 [768, 3072], P('col', 'row')
- grad_expand_bias: float32 [3072], P('row')
- grad_shrink_weight: float32 [768, 3072], P('col', 'row')
- grad_shrink_bias: float32 [768], P('col')
The draws below stay inside these ranges and needn't reach their ends.
All inputs are finite; a program needn't handle non-finite values.
Results may differ from the reference program's by a relative error of at most 0.015.
Values may be sent and summed in bfloat16 or wider, within the bound.
No kernel may reach another device: no remote copies, remote signals or barrier semaphores. Data moves between devices by JAX's collectives and lax.ppermute only.
A program may use at most 128 MiB of HBM per device.

```python
import jax
import jax.numpy as jnp
from jax import lax

D = 768
H = 12
HD = 64
FF = 3072
SEQ = 197
IMG_DEV = 3
TG = 2364
TOKENS = 4728
N_DP = 2
N_COL = 4


def shard_levels(own_key, extent, shards, least, largest):
    loudness = 1.0
    for position, blocks in shards:
        heights = jax.random.uniform(jax.random.fold_in(jax.random.fold_in(own_key, 6), position), (blocks,), jnp.float32, least / len(shards), largest / len(shards))
        loudness = loudness * jnp.repeat(jnp.exp(heights), extent[position] // blocks).reshape((-1,) + (1,) * (len(extent) - 1 - position))
    return loudness


def bell_draw(key, shape, spread, most, split=(), dtype=jnp.bfloat16):
    entries = spread * jax.random.normal(key, shape, jnp.float32)
    if split:
        entries = entries * shard_levels(key, shape, split, -0.22, 0.18)
    return jnp.clip(entries, -most, most).astype(dtype)


def setup_inputs(seed: int = 0) -> dict:
    streams_of = jax.random.split(jax.random.key(seed), 18)
    tokens = bell_draw(streams_of[0], (TOKENS, D), 1.0, 6.0, ((0, 8),))
    attn_gain = jnp.clip(1.0 + 0.1 * jax.random.normal(streams_of[1], (D,), jnp.float32), 0.5, 1.5)
    attn_shift = bell_draw(streams_of[2], (D,), 0.5, 3.0, (), jnp.float32)
    query_weight = bell_draw(streams_of[3], (D, D), D ** -0.5, 0.21875, ((0, 4), (1, 4)))
    key_weight = bell_draw(streams_of[4], (D, D), D ** -0.5, 0.21875, ((0, 4), (1, 4)))
    value_weight = bell_draw(streams_of[5], (D, D), D ** -0.5, 0.21875, ((0, 4), (1, 4)))
    query_bias = bell_draw(streams_of[6], (D,), 0.5, 3.0, ((0, 4),), jnp.float32)
    value_bias = bell_draw(streams_of[7], (D,), 0.5, 3.0, ((0, 4),), jnp.float32)
    proj_weight = bell_draw(streams_of[8], (D, D), (D // 8) ** -0.5, 0.625, ((0, 4), (1, 4)))
    proj_bias = bell_draw(streams_of[9], (D,), 0.5, 3.0, ((0, 4),), jnp.float32)
    mlp_gain = jnp.clip(1.0 + 0.1 * jax.random.normal(streams_of[10], (D,), jnp.float32), 0.5, 1.5)
    mlp_shift = bell_draw(streams_of[11], (D,), 0.5, 3.0, (), jnp.float32)
    expand_weight = bell_draw(streams_of[12], (D, FF), D ** -0.5, 0.21875, ((0, 4), (1, 4)))
    expand_bias = bell_draw(streams_of[13], (FF,), 0.5, 3.0, ((0, 4),), jnp.float32)
    shrink_weight = bell_draw(streams_of[14], (D, FF), FF ** -0.5, 0.109375, ((0, 4), (1, 4)))
    shrink_bias = bell_draw(streams_of[15], (D,), 0.5, 3.0, ((0, 4),), jnp.float32)
    cotangent = bell_draw(streams_of[16], (TOKENS, D), 1.0, 6.0, ((0, 8),))
    return {"tokens": tokens, "attn_gain": attn_gain, "attn_shift": attn_shift, "query_weight": query_weight, "key_weight": key_weight, "value_weight": value_weight, "query_bias": query_bias, "value_bias": value_bias, "proj_weight": proj_weight, "proj_bias": proj_bias, "mlp_gain": mlp_gain, "mlp_shift": mlp_shift, "expand_weight": expand_weight, "expand_bias": expand_bias, "shrink_weight": shrink_weight, "shrink_bias": shrink_bias, "cotangent": cotangent}


EPS = 1e-06

def normalize(values, norm_gain, norm_shift):
    mean_part = lax.optimization_barrier(jnp.mean(values, axis=-1, keepdims=True))
    square_part = lax.optimization_barrier(jnp.mean(values * values, axis=-1, keepdims=True))
    inverse = lax.rsqrt(square_part - mean_part * mean_part + EPS)
    centred = (values - mean_part) * inverse
    return (centred, inverse, centred * norm_gain + norm_shift)

def norm_back(grad_normed, centred, inverse, norm_gain):
    scaled = grad_normed * norm_gain
    first_mean = lax.optimization_barrier(jnp.mean(scaled, axis=-1, keepdims=True))
    second_mean = lax.optimization_barrier(jnp.mean(scaled * centred, axis=-1, keepdims=True))
    return inverse * (scaled - first_mean - centred * second_mean)

def gelu_parts(pre_act):
    cdf_value = 0.5 * (1.0 + jax.scipy.special.erf(pre_act * 0.7071067811865476))
    density = jnp.exp(-0.5 * pre_act * pre_act) * 0.3989422804014327
    return (pre_act * cdf_value, cdf_value + pre_act * density)

def scores_of(query_rows, key_rows):
    return jnp.einsum('iqhd,ikhd->ihqk', query_rows.astype(jnp.float32), key_rows.astype(jnp.float32)) * HD ** (-0.5)

def group_pass(tokens_block, cot_block, weights):
    attn_gain, attn_shift, query_weight, key_weight, value_weight, query_bias, value_bias, proj_weight, proj_bias, mlp_gain, mlp_shift, expand_weight, expand_bias, shrink_weight, shrink_bias = weights
    shape_four = (IMG_DEV * N_COL, SEQ, H, HD)
    inputs = tokens_block.astype(jnp.float32)
    centred_one, inverse_one, normed_one = normalize(inputs, attn_gain, attn_shift)
    first_in = normed_one.astype(jnp.bfloat16)
    query_rows = (jnp.dot(first_in, query_weight, preferred_element_type=jnp.float32) + query_bias).astype(jnp.bfloat16)
    key_rows = jnp.dot(first_in, key_weight, preferred_element_type=jnp.float32).astype(jnp.bfloat16)
    value_rows = (jnp.dot(first_in, value_weight, preferred_element_type=jnp.float32) + value_bias).astype(jnp.bfloat16)
    query_four = query_rows.reshape(shape_four)
    key_four = key_rows.reshape(shape_four)
    value_four = value_rows.reshape(shape_four)
    scores = scores_of(query_four, key_four)
    log_total = jnp.log(lax.optimization_barrier(jnp.sum(jnp.exp(scores), axis=-1, keepdims=True)))
    attn_probs = jnp.exp(scores - log_total).astype(jnp.bfloat16)
    attended = jnp.einsum('ihqk,ikhd->iqhd', attn_probs.astype(jnp.float32), value_four.astype(jnp.float32))
    attended = attended.astype(jnp.bfloat16).reshape(TG, D)
    mid = inputs + jnp.dot(attended, proj_weight, preferred_element_type=jnp.float32) + proj_bias
    centred_two, inverse_two, normed_two = normalize(mid, mlp_gain, mlp_shift)
    second_in = normed_two.astype(jnp.bfloat16)
    pre_act = jnp.dot(second_in, expand_weight, preferred_element_type=jnp.float32) + expand_bias
    activ, slope = gelu_parts(pre_act)
    hidden = activ.astype(jnp.bfloat16)
    output = (mid + jnp.dot(hidden, shrink_weight.T, preferred_element_type=jnp.float32) + shrink_bias).astype(jnp.bfloat16)
    grad_out = cot_block.astype(jnp.float32)
    grad_shrink_bias = lax.optimization_barrier(jnp.sum(grad_out, axis=0))
    grad_shrink_weight = jnp.dot(cot_block.T, hidden, preferred_element_type=jnp.float32)
    grad_pre = jnp.dot(cot_block, shrink_weight, preferred_element_type=jnp.float32) * slope
    grad_expand_bias = lax.optimization_barrier(jnp.sum(grad_pre, axis=0))
    grad_pre_b = grad_pre.astype(jnp.bfloat16)
    grad_expand_weight = jnp.dot(second_in.T, grad_pre_b, preferred_element_type=jnp.float32)
    grad_normed_two = jnp.dot(grad_pre_b, expand_weight.T, preferred_element_type=jnp.float32)
    grad_mlp_gain = lax.optimization_barrier(jnp.sum(grad_normed_two * centred_two, axis=0))
    grad_mlp_shift = lax.optimization_barrier(jnp.sum(grad_normed_two, axis=0))
    grad_mid = grad_out + norm_back(grad_normed_two, centred_two, inverse_two, mlp_gain)
    grad_proj_bias = lax.optimization_barrier(jnp.sum(grad_mid, axis=0))
    grad_mid_b = grad_mid.astype(jnp.bfloat16)
    grad_proj_weight = jnp.dot(attended.T, grad_mid_b, preferred_element_type=jnp.float32)
    grad_att = jnp.dot(grad_mid_b, proj_weight.T, preferred_element_type=jnp.float32).astype(jnp.bfloat16).reshape(shape_four)
    attn_full = jnp.exp(scores_of(query_four, key_four) - log_total)
    grad_value = jnp.einsum('ihqk,iqhd->ikhd', attn_probs.astype(jnp.float32), grad_att.astype(jnp.float32))
    grad_weights = jnp.einsum('iqhd,ikhd->ihqk', grad_att.astype(jnp.float32), value_four.astype(jnp.float32))
    row_delta = lax.optimization_barrier(jnp.sum(attn_full * grad_weights, axis=-1, keepdims=True))
    grad_scores = (attn_full * (grad_weights - row_delta) * HD ** (-0.5)).astype(jnp.bfloat16)
    grad_query = jnp.einsum('ihqk,ikhd->iqhd', grad_scores.astype(jnp.float32), key_four.astype(jnp.float32)).reshape(TG, D)
    grad_key = jnp.einsum('ihqk,iqhd->ikhd', grad_scores.astype(jnp.float32), query_four.astype(jnp.float32)).reshape(TG, D)
    grad_value = grad_value.reshape(TG, D)
    grad_query_bias = lax.optimization_barrier(jnp.sum(grad_query, axis=0))
    grad_value_bias = lax.optimization_barrier(jnp.sum(grad_value, axis=0))
    grad_query_b = grad_query.astype(jnp.bfloat16)
    grad_key_b = grad_key.astype(jnp.bfloat16)
    grad_value_b = grad_value.astype(jnp.bfloat16)
    grad_query_weight = jnp.dot(first_in.T, grad_query_b, preferred_element_type=jnp.float32)
    grad_key_weight = jnp.dot(first_in.T, grad_key_b, preferred_element_type=jnp.float32)
    grad_value_weight = jnp.dot(first_in.T, grad_value_b, preferred_element_type=jnp.float32)
    grad_normed_one = jnp.dot(grad_query_b, query_weight.T, preferred_element_type=jnp.float32) + jnp.dot(grad_key_b, key_weight.T, preferred_element_type=jnp.float32) + jnp.dot(grad_value_b, value_weight.T, preferred_element_type=jnp.float32)
    grad_attn_gain = lax.optimization_barrier(jnp.sum(grad_normed_one * centred_one, axis=0))
    grad_attn_shift = lax.optimization_barrier(jnp.sum(grad_normed_one, axis=0))
    grad_tokens = (grad_mid + norm_back(grad_normed_one, centred_one, inverse_one, attn_gain)).astype(jnp.bfloat16)
    grads = (grad_attn_gain, grad_attn_shift, grad_query_weight, grad_key_weight, grad_value_weight, grad_query_bias, grad_value_bias, grad_proj_weight, grad_proj_bias, grad_mlp_gain, grad_mlp_shift, grad_expand_weight, grad_expand_bias, grad_shrink_weight, grad_shrink_bias)
    return (output, grad_tokens, grads)

def add_pair(left, right):
    return left + right

def zeros_like_float(weight):
    return jnp.zeros(weight.shape, jnp.float32)

def reference(tokens, attn_gain, attn_shift, query_weight, key_weight, value_weight, query_bias, value_bias, proj_weight, proj_bias, mlp_gain, mlp_shift, expand_weight, expand_bias, shrink_weight, shrink_bias, cotangent):
    weights = (attn_gain, attn_shift, query_weight, key_weight, value_weight, query_bias, value_bias, proj_weight, proj_bias, mlp_gain, mlp_shift, expand_weight, expand_bias, shrink_weight, shrink_bias)

    def step(carry, blocks):
        output, grad_tokens, grads = group_pass(blocks[0], blocks[1], weights)
        return (jax.tree.map(add_pair, carry, grads), (output, grad_tokens))
    start = jax.tree.map(zeros_like_float, weights)
    totals, (outputs, grads_in) = lax.scan(step, start, (tokens.reshape(N_DP, TG, D), cotangent.reshape(N_DP, TG, D)))
    return (outputs.reshape(TOKENS, D), grads_in.reshape(TOKENS, D), totals[0], totals[1], totals[2], totals[3], totals[4], totals[5], totals[6], totals[7], totals[8], totals[9], totals[10], totals[11], totals[12], totals[13], totals[14])
```

```python
import jax
import jax.numpy as jnp
from jax import lax
from jax.sharding import PartitionSpec as P

HD = 64
SEQ = 197
PAD = 208
EPS = 1e-06
BF = jnp.bfloat16
F32 = jnp.float32


def mirrored(index, size):
    out, step = 0, 1
    while step < size:
        out = out * 2 + (index // step) % 2
        step *= 2
    return out


class Grid:
    def __init__(self):
        self.rows = lax.axis_size("row")
        self.cols = lax.axis_size("col")
        self.dps = lax.axis_size("dp")
        assert self.rows == self.cols
        self.row = lax.axis_index("row")
        self.col = lax.axis_index("col")
        self.dp = lax.axis_index("dp")
        self.mirror = [mirrored(c, self.cols) for c in range(self.cols)]

    def fetch(self, array, flip):
        pairs = []
        for r in range(self.rows):
            for c in range(self.cols):
                source = (r ^ self.mirror[c]) * self.cols + (c ^ flip)
                pairs.append((source, r * self.cols + c))
        return lax.ppermute(array, ("row", "col"), pairs)

    def give(self, array, flip):
        pairs = []
        for r in range(self.rows):
            for c in range(self.cols):
                target = (r ^ self.mirror[c]) * self.cols + (c ^ flip)
                pairs.append((r * self.cols + c, target))
        return lax.ppermute(array, ("row", "col"), pairs)

    def swap(self, array, axis, flip):
        size = lax.axis_size(axis)
        return lax.ppermute(array, axis, [(i, i ^ flip) for i in range(size)])


def gather_block(grid, shard):
    half = shard.shape[0] // 2
    mine = lax.dynamic_slice_in_dim(shard, (grid.dp % 2) * half, half, 0)
    width = shard.shape[1]
    full = jnp.zeros((grid.cols * 2 * half, width), shard.dtype)
    for flip in range(grid.cols):
        here = grid.fetch(mine, flip)
        there = grid.swap(here, "dp", 1)
        base = (grid.col ^ flip) * 2 * half
        full = lax.dynamic_update_slice_in_dim(full, here, base + (grid.dp % 2) * half, 0)
        full = lax.dynamic_update_slice_in_dim(full, there, base + (1 - grid.dp % 2) * half, 0)
    return full


def reduce_block(grid, partial):
    half = partial.shape[0] // (2 * grid.cols)
    parts = partial.reshape(grid.cols, 2, half, partial.shape[1])
    own = lax.dynamic_index_in_dim(parts, grid.dp % 2, 1, keepdims=False)
    other = lax.dynamic_index_in_dim(parts, 1 - grid.dp % 2, 1, keepdims=False)
    total = None
    for flip in range(grid.cols):
        col = grid.col ^ flip
        away = lax.dynamic_index_in_dim(other, col, 0, keepdims=False)
        stay = lax.dynamic_index_in_dim(own, col, 0, keepdims=False)
        pair = stay.astype(F32) + grid.swap(away, "dp", 1).astype(F32)
        got = grid.give(pair.astype(BF), flip).astype(F32)
        total = got if total is None else total + got
    step = 2
    while step < grid.dps:
        total = total + grid.swap(total.astype(BF), "dp", step).astype(F32)
        step *= 2
    total = total.astype(BF)
    back = grid.swap(total, "dp", 1)
    first = grid.dp % 2 == 0
    return jnp.concatenate([jnp.where(first, total, back), jnp.where(first, back, total)], 0).astype(F32)


def sum_cols(grid, partial):
    half = partial.shape[1] // 2
    first = grid.col % 2 == 0
    left, right = partial[:, :half], partial[:, half:]
    mine = jnp.where(first, left, right)
    away = jnp.where(first, right, left)
    mine = (mine.astype(F32) + grid.swap(away, "col", 1).astype(F32)).astype(BF)
    step = 2
    while step < grid.cols:
        mine = (mine.astype(F32) + grid.swap(mine, "col", step).astype(F32)).astype(BF)
        step *= 2
    other = grid.swap(mine, "col", 1)
    return jnp.concatenate([jnp.where(first, mine, other), jnp.where(first, other, mine)], 1).astype(F32)


def normalize(values, norm_gain, norm_shift):
    mean_part = jnp.mean(values, axis=-1, keepdims=True)
    square_part = jnp.mean(values * values, axis=-1, keepdims=True)
    inverse = lax.rsqrt(square_part - mean_part * mean_part + EPS)
    centred = (values - mean_part) * inverse
    return (centred, inverse, centred * norm_gain + norm_shift)


def norm_back(grad_normed, centred, inverse, norm_gain):
    scaled = grad_normed * norm_gain
    first_mean = jnp.mean(scaled, axis=-1, keepdims=True)
    second_mean = jnp.mean(scaled * centred, axis=-1, keepdims=True)
    return inverse * (scaled - first_mean - centred * second_mean)


def gelu_parts(pre_act):
    cdf_value = 0.5 * (1.0 + jax.scipy.special.erf(pre_act * 0.7071067811865476))
    density = jnp.exp(-0.5 * pre_act * pre_act) * 0.3989422804014327
    return (pre_act * cdf_value, cdf_value + pre_act * density)


def dot(left, right, contract):
    return lax.dot_general(left, right, ((contract[:1], contract[1:]), ((), ())), preferred_element_type=F32)


def padded(rows):
    images = rows.shape[0] // SEQ
    rows = rows.reshape(images, SEQ, rows.shape[1])
    return jnp.pad(rows, ((0, 0), (0, PAD - SEQ), (0, 0))).reshape(images * PAD, -1)


def unpadded(rows):
    images = rows.shape[0] // PAD
    return rows.reshape(images, PAD, -1)[:, :SEQ].reshape(images * SEQ, -1)


def on_device(
    tokens,
    attn_gain,
    attn_shift,
    query_weight,
    key_weight,
    value_weight,
    query_bias,
    value_bias,
    proj_weight,
    proj_bias,
    mlp_gain,
    mlp_shift,
    expand_weight,
    expand_bias,
    shrink_weight,
    shrink_bias,
    cotangent,
):
    grid = Grid()
    wide = query_weight.shape[1]
    model = tokens.shape[1]
    hidden_here = expand_weight.shape[1]

    joined = gather_block(grid, jnp.concatenate([query_weight, key_weight, value_weight], axis=1))
    proj_t = gather_block(grid, proj_weight.T)
    expand = gather_block(grid, expand_weight)
    shrink = gather_block(grid, shrink_weight)
    biases = grid.fetch(jnp.concatenate([query_bias, value_bias, expand_bias]), 0)
    q_bias, v_bias, e_bias = biases[:wide], biases[wide : 2 * wide], biases[2 * wide :]
    joined_bias = jnp.concatenate([q_bias, jnp.zeros_like(q_bias), v_bias])

    def spread(bias):
        own = jnp.arange(model) // bias.shape[0] == grid.col
        return jnp.where(own, jnp.tile(bias, grid.cols), 0.0)

    inputs = padded(tokens.astype(F32))
    cot = padded(cotangent)
    rows = inputs.shape[0]
    images = rows // PAD
    centred_one, inverse_one, normed_one = normalize(inputs, attn_gain, attn_shift)
    first_in = normed_one.astype(BF)
    projected = (dot(first_in, joined, (1, 0)) + joined_bias).astype(BF)
    four = (images, PAD, wide // HD, HD)
    query, key, value = (projected[:, i * wide : (i + 1) * wide].reshape(four) for i in range(3))
    scores = jnp.einsum("iqhd,ikhd->ihqk", query, key, preferred_element_type=F32) * HD**-0.5
    is_key = jnp.arange(PAD) < SEQ
    log_total = jnp.log(jnp.sum(jnp.where(is_key, jnp.exp(scores), 0.0), axis=-1, keepdims=True))
    attn_full = jnp.where(is_key, jnp.exp(scores - log_total), 0.0)
    attn_probs = attn_full.astype(BF)
    attended = jnp.einsum("ihqk,ikhd->iqhd", attn_probs, value, preferred_element_type=F32)
    attended = attended.astype(BF).reshape(rows, wide)
    mid = inputs + sum_cols(grid, (dot(attended, proj_t, (1, 1)) + spread(proj_bias)).astype(BF))

    centred_two, inverse_two, normed_two = normalize(mid, mlp_gain, mlp_shift)
    second_in = normed_two.astype(BF)
    pre_act = dot(second_in, expand, (1, 0)) + e_bias
    activ, slope = gelu_parts(pre_act)
    hidden = activ.astype(BF)
    grad_pre = dot(cot, shrink, (1, 0)) * slope
    grad_pre_b = grad_pre.astype(BF)
    grad_normed_two = sum_cols(grid, dot(grad_pre_b, expand, (1, 1)).astype(BF))
    output = mid + sum_cols(grid, (dot(hidden, shrink, (1, 1)) + spread(shrink_bias)).astype(BF))
    grad_shrink = reduce_block(grid, dot(cot, hidden, (0, 0)).astype(BF))
    grad_expand = reduce_block(grid, dot(second_in, grad_pre_b, (0, 0)).astype(BF))

    grad_out = cot.astype(F32)
    grad_mid = grad_out + norm_back(grad_normed_two, centred_two, inverse_two, mlp_gain)
    grad_mid_b = grad_mid.astype(BF)
    grad_proj = reduce_block(grid, dot(grad_mid_b, attended, (0, 0)).astype(BF)).T
    grad_att = dot(grad_mid_b, proj_t, (1, 0)).astype(BF).reshape(four)
    grad_value = jnp.einsum("ihqk,iqhd->ikhd", attn_probs, grad_att, preferred_element_type=F32)
    grad_weights = jnp.einsum("iqhd,ikhd->ihqk", grad_att, value, preferred_element_type=F32)
    row_delta = jnp.sum(attn_full * grad_weights, axis=-1, keepdims=True)
    grad_scores = (attn_full * (grad_weights - row_delta) * HD**-0.5).astype(BF)
    grad_query = jnp.einsum("ihqk,ikhd->iqhd", grad_scores, key, preferred_element_type=F32)
    grad_key = jnp.einsum("ihqk,iqhd->ikhd", grad_scores, query, preferred_element_type=F32)
    grad_joined = jnp.concatenate([g.reshape(rows, wide) for g in (grad_query, grad_key, grad_value)], axis=1)
    grad_joined_b = grad_joined.astype(BF)
    grad_weight = reduce_block(grid, dot(first_in, grad_joined_b, (0, 0)).astype(BF))
    grad_normed_one = sum_cols(grid, dot(grad_joined_b, joined, (1, 1)).astype(BF))
    grad_tokens = grad_mid + norm_back(grad_normed_one, centred_one, inverse_one, attn_gain)

    whole = lax.psum(
        jnp.stack(
            [
                jnp.sum(grad_normed_one * centred_one, axis=0),
                jnp.sum(grad_normed_one, axis=0),
                jnp.sum(grad_normed_two * centred_two, axis=0),
                jnp.sum(grad_normed_two, axis=0),
                jnp.sum(grad_mid, axis=0),
                jnp.sum(grad_out, axis=0),
            ]
        ),
        ("dp", "row"),
    )
    joined_sums = jnp.sum(grad_joined, axis=0)
    blocks = jnp.concatenate([joined_sums[:wide], joined_sums[2 * wide :], jnp.sum(grad_pre, axis=0)])
    blocks = lax.psum(grid.give(blocks, 0), ("dp", "col"))

    def own_columns(vector):
        width = vector.shape[0] // grid.cols
        return lax.dynamic_slice_in_dim(vector, grid.col * width, width, 0)

    return (
        unpadded(output.astype(BF)),
        unpadded(grad_tokens.astype(BF)),
        whole[0],
        whole[1],
        grad_weight[:, :wide],
        grad_weight[:, wide : 2 * wide],
        grad_weight[:, 2 * wide :],
        blocks[:wide],
        blocks[wide : 2 * wide],
        grad_proj,
        own_columns(whole[4]),
        whole[2],
        whole[3],
        grad_expand,
        blocks[2 * wide :],
        grad_shrink,
        own_columns(whole[5]),
    )


def solution(mesh):
    placed = (
        P(("dp", "row"), None),
        P(),
        P(),
        P("col", "row"),
        P("col", "row"),
        P("col", "row"),
        P("row"),
        P("row"),
        P("row", "col"),
        P("col"),
        P(),
        P(),
        P("col", "row"),
        P("row"),
        P("col", "row"),
        P("col"),
        P(("dp", "row"), None),
    )
    return jax.shard_map(
        on_device,
        mesh=mesh,
        in_specs=placed,
        out_specs=(
            P(("dp", "row"), None),
            P(("dp", "row"), None),
            P(),
            P(),
            P("col", "row"),
            P("col", "row"),
            P("col", "row"),
            P("row"),
            P("row"),
            P("row", "col"),
            P("col"),
            P(),
            P(),
            P("col", "row"),
            P("row"),
            P("col", "row"),
            P("col"),
        ),
        check_vma=False,
    )
```

```python
import jax
import jax.numpy as jnp
from jax import lax
from jax.experimental import pallas as pl
from jax.experimental.pallas import tpu as pltpu
from jax.sharding import PartitionSpec as P

HD = 64
SEQ = 197
PAD = 208
LANES = 128
EPS = 1e-06
BF = jnp.bfloat16
F32 = jnp.float32


def mirrored(index, size):
    out, step = 0, 1
    while step < size:
        out = out * 2 + (index // step) % 2
        step *= 2
    return out


class Grid:
    def __init__(self):
        self.rows = lax.axis_size("row")
        self.cols = lax.axis_size("col")
        self.dps = lax.axis_size("dp")
        assert self.rows == self.cols
        self.row = lax.axis_index("row")
        self.col = lax.axis_index("col")
        self.dp = lax.axis_index("dp")
        self.mirror = [mirrored(c, self.cols) for c in range(self.cols)]
        self.block = self.row ^ jnp.array(self.mirror, jnp.int32)[self.col]
        self.ids = jnp.stack([self.col, self.dp % 2]).astype(jnp.int32)

    def fetch(self, array, flip):
        pairs = []
        for r in range(self.rows):
            for c in range(self.cols):
                source = (r ^ self.mirror[c]) * self.cols + (c ^ flip)
                pairs.append((source, r * self.cols + c))
        return lax.ppermute(array, ("row", "col"), pairs)

    def give(self, array, flip):
        pairs = []
        for r in range(self.rows):
            for c in range(self.cols):
                target = (r ^ self.mirror[c]) * self.cols + (c ^ flip)
                pairs.append((r * self.cols + c, target))
        return lax.ppermute(array, ("row", "col"), pairs)

    def swap(self, array, axis, flip):
        size = lax.axis_size(axis)
        return lax.ppermute(array, axis, [(i, i ^ flip) for i in range(size)])


def after(value, *others):
    return lax.optimization_barrier((value, *others))[0]


def gather_block(grid, shard, first=None):
    half = shard.shape[0] // 2
    mine = lax.dynamic_slice_in_dim(shard, (grid.dp % 2) * half, half, 0)
    if first is not None:
        mine = after(mine, first)
    here = [grid.fetch(mine, flip) for flip in range(grid.cols)]
    there = [grid.swap(jnp.stack(here[i : i + 2]), "dp", 1) for i in range(0, grid.cols, 2)]
    return here, there


def reduce_block(grid, stay, away):
    got = grid.swap(away, "dp", 1)
    pair = (stay.astype(F32) + got.astype(F32)).astype(BF)
    total = None
    for flip in range(grid.cols):
        part = grid.give(pair[flip], flip).astype(F32)
        total = part if total is None else total + part
    step = 2
    while step < grid.dps:
        total = total + grid.swap(total.astype(BF), "dp", step).astype(F32)
        step *= 2
    total = total.astype(BF)
    back = grid.swap(total, "dp", 1)
    first = grid.dp % 2 == 0
    return jnp.concatenate([jnp.where(first, total, back), jnp.where(first, back, total)], 0).astype(F32)


def sum_cols(grid, mine, away):
    mine = mine + grid.swap(away, "col", 1)
    step = 2
    while step < grid.cols:
        mine = mine + grid.swap(mine, "col", step)
        step *= 2
    return mine, grid.swap(mine, "col", 1)


def sum_all(grid, array):
    for axis in ("col", "row", "dp"):
        step = 1
        while step < lax.axis_size(axis):
            array = array + grid.swap(array, axis, step)
            step *= 2
    return array


def sum_tokens(grid, array):
    for axis in ("row", "dp"):
        step = 1
        while step < lax.axis_size(axis):
            array = array + grid.swap(array, axis, step)
            step *= 2
    return array


def dot(left, right, contract):
    return lax.dot_general(left, right, ((contract[:1], contract[1:]), ((), ())), preferred_element_type=F32)


def normalize(values):
    mean_part = jnp.mean(values, axis=-1, keepdims=True)
    square_part = jnp.mean(values * values, axis=-1, keepdims=True)
    inverse = lax.rsqrt(square_part - mean_part * mean_part + EPS)
    return (values - mean_part) * inverse, inverse


def norm_back(grad_normed, centred, inverse, norm_gain):
    scaled = grad_normed * norm_gain
    first_mean = jnp.mean(scaled, axis=-1, keepdims=True)
    second_mean = jnp.mean(scaled * centred, axis=-1, keepdims=True)
    return inverse * (scaled - first_mean - centred * second_mean)


def gelu_parts(pre_act):
    cdf_value = 0.5 * (1.0 + lax.erf(pre_act * 0.7071067811865476))
    density = jnp.exp(-0.5 * pre_act * pre_act) * 0.3989422804014327
    return (pre_act * cdf_value, cdf_value + pre_act * density)


def columns_sum(values):
    return jnp.sum(values, axis=0, keepdims=True)


def low_lanes(shape):
    return lax.broadcasted_iota(jnp.int32, shape, len(shape) - 1) % LANES < HD


def low(values):
    return jnp.where(low_lanes(values.shape), values, jnp.zeros_like(values))


def high(values):
    return jnp.where(low_lanes(values.shape), jnp.zeros_like(values), values)


def place(ids, here, there, full):
    half = here[0].shape[0]
    pairs = [(ref, flip, ids[1]) for flip, ref in enumerate(here)]
    for i, ref in enumerate(there):
        pairs += [(ref.at[j], 2 * i + j, 1 - ids[1]) for j in range(2)]
    for ref, flip, side in pairs:
        start = pl.multiple_of(((ids[0] ^ flip) * 2 + side) * half, half)
        full[pl.ds(start, half), :] = ref[...]


def split_halves(ids, values, mine, away):
    half = values.shape[1] // 2
    left, right = values[:, :half], values[:, half:]
    first = ids[0] % 2 == 0
    mine[...] = jnp.where(first, left, right)
    away[...] = jnp.where(first, right, left)


def join_halves(ids, mine, other):
    first = ids[0] % 2 == 0
    a, b = mine[...].astype(F32), other[...].astype(F32)
    return jnp.concatenate([jnp.where(first, a, b), jnp.where(first, b, a)], axis=1)


def enter_kernel(tokens, cot, gain, shift, tokens_out, first_out, cot_out, sums):
    images = tokens.shape[0] // SEQ
    total = jnp.zeros((1, tokens.shape[1]), F32)
    for i in range(images):
        blank = jnp.zeros((PAD - SEQ, tokens.shape[1]), F32)
        here = pl.ds(i * PAD, PAD)
        rows = jnp.concatenate([tokens[pl.ds(i * SEQ, SEQ), :].astype(F32), blank], axis=0)
        tokens_out[here, :] = rows.astype(BF)
        centred, _ = normalize(rows)
        first_out[here, :] = (centred * gain[...] + shift[...]).astype(BF)
        rows = jnp.concatenate([cot[pl.ds(i * SEQ, SEQ), :].astype(F32), blank], axis=0)
        cot_out[here, :] = rows.astype(BF)
        total += columns_sum(rows)
    sums[...] = total


def attend_kernel(ids, first, h0, h1, h2, h3, t0, t1, bias, proj_bias, full, proj, joined, attended, probs, mine, away):
    @pl.when(pl.program_id(0) == 0)
    def _():
        place(ids, (h0, h1, h2, h3), (t0, t1), full)
        one, two, three = (full[:, i * LANES : (i + 1) * LANES].astype(F32) for i in (1, 3, 5))
        is_low = low_lanes(one.shape)
        proj[:, :LANES] = jnp.where(is_low, pltpu.roll(one, HD, 1), two).astype(BF)
        proj[:, LANES:] = low(pltpu.roll(three, HD, 1)).astype(BF)

    rows = (dot(first[...], full[...], (1, 0)) + bias[...]).astype(BF)
    query = rows[:, : 2 * LANES] * jnp.asarray(HD**-0.5, BF)
    joined[:, : 2 * LANES] = query
    joined[:, 2 * LANES :] = rows[:, 2 * LANES :]
    key, value = rows[:, 2 * LANES : 4 * LANES], rows[:, 4 * LANES :]
    is_key = lax.broadcasted_iota(jnp.int32, (PAD, PAD), 1) < SEQ
    outs = []
    for head in range(3):
        lanes = slice(head // 2 * LANES, (head // 2 + 1) * LANES)
        part = high if head == 1 else low
        scores = dot(query[:, lanes], part(key[:, lanes]), (1, 1))
        scores = jnp.where(is_key, scores, -1e30)
        weights = jnp.exp(scores - jnp.max(scores, axis=-1, keepdims=True))
        weights = (weights * (1.0 / jnp.sum(weights, axis=-1, keepdims=True))).astype(BF)
        probs[head] = weights
        outs.append(dot(weights, part(value[:, lanes]), (1, 0)))
    result = jnp.concatenate([outs[0] + outs[1], outs[2]], axis=1).astype(BF)
    attended[...] = result
    split_halves(ids, (dot(result, proj[...], (1, 1)) + proj_bias[...]).astype(BF), mine, away)


def mlp_kernel(
    ids, tokens, one, two, cot, gain, shift, bias, e0, e1, e2, e3, f0, f1, s0, s1, s2, s3, u0, u1,
    shrink, mid_out, second_out, hidden_out, pre_out, mine, away, sums, expand
):
    @pl.when(pl.program_id(0) == 0)
    def _():
        place(ids, (e0, e1, e2, e3), (f0, f1), expand)
        place(ids, (s0, s1, s2, s3), (u0, u1), shrink)
        sums[...] = jnp.zeros_like(sums)

    mid = tokens[...].astype(F32) + join_halves(ids, one, two)
    mid_out[...] = mid
    centred, _ = normalize(mid)
    second = (centred * gain[...] + shift[...]).astype(BF)
    second_out[...] = second
    activ, slope = gelu_parts(dot(second, expand[...], (1, 0)) + bias[...])
    hidden_out[...] = activ.astype(BF)
    grad_pre = dot(cot[...], shrink[...], (1, 0)) * slope
    sums[...] += columns_sum(grad_pre)
    grad_pre = grad_pre.astype(BF)
    pre_out[...] = grad_pre
    split_halves(ids, dot(grad_pre, expand[...], (1, 1)).astype(BF), mine, away)


def shrink_kernel(ids, hidden, shrink, bias, mine, away):
    split_halves(ids, (dot(hidden[...], shrink[...], (1, 1)) + bias[...]).astype(BF), mine, away)


def deal(ids, full, stay, away):
    half = stay.shape[1]
    for flip in range(stay.shape[0]):
        base = (ids[0] ^ flip) * 2
        stay[flip] = full[pl.ds(pl.multiple_of((base + ids[1]) * half, half), half), :]
        away[flip] = full[pl.ds(pl.multiple_of((base + 1 - ids[1]) * half, half), half), :]


def outer_kernel(ids, left, right, stay, away, full):
    full[...] = dot(left[...], right[...], (0, 0)).astype(BF)
    deal(ids, full, stay, away)


def joined_outer_kernel(ids, first, joined, grad_mid, attended, stay, away, full):
    full[...] = dot(first[...], joined[...], (0, 0)).astype(BF)
    other = dot(grad_mid[...], attended[...], (0, 0))
    turned = (pltpu.roll(other[:, :LANES], HD, 1), other[:, :LANES], pltpu.roll(other[:, LANES:], HD, 1))
    for i, values in enumerate(turned):
        lanes = pl.ds((2 * i + 1) * LANES, LANES)
        is_low = low_lanes(values.shape)
        full[:, lanes] = jnp.where(is_low, full[:, lanes].astype(F32), values).astype(BF)
    deal(ids, full, stay, away)


def attend_back_kernel(
    ids, one, two, mid, cot, gain, full, proj, joined, probs,
    grad_mid_out, grad_mid_b_out, grad_joined_out, mine, away, sums
):
    @pl.when(pl.program_id(0) == 0)
    def _():
        sums[...] = jnp.zeros_like(sums)

    grad_normed = join_halves(ids, one, two)
    centred, inverse = normalize(mid[...])
    grad_mid = cot[...].astype(F32) + norm_back(grad_normed, centred, inverse, gain[...])
    grad_mid_out[...] = grad_mid
    grad_mid_b = grad_mid.astype(BF)
    grad_mid_b_out[...] = grad_mid_b
    grad_att = dot(grad_mid_b, proj[...], (1, 0)).astype(BF)
    query, key, value = (joined[:, i * 2 * LANES : (i + 1) * 2 * LANES] for i in range(3))
    queries, keys, values = [], [], []
    for head in range(3):
        lanes = slice(head // 2 * LANES, (head // 2 + 1) * LANES)
        part = high if head == 1 else low
        weights = probs[head]
        wide = weights.astype(F32)
        grad_weights = dot(grad_att[:, lanes], part(value[:, lanes]), (1, 1))
        row_delta = jnp.sum(wide * grad_weights, axis=-1, keepdims=True)
        grad_scores = (wide * (grad_weights - row_delta)).astype(BF)
        queries.append(dot(grad_scores, part(key[:, lanes]), (1, 0)))
        keys.append(dot(grad_scores, part(query[:, lanes]), (0, 0)))
        values.append(dot(weights, part(grad_att[:, lanes]), (0, 0)))
    scale = HD**-0.5
    result = jnp.concatenate(
        [(queries[0] + queries[1]) * scale, queries[2] * scale, keys[0] + keys[1], keys[2], values[0] + values[1], values[2]],
        axis=1,
    )
    sums[0:1, :] += columns_sum(grad_normed * centred)
    sums[1:2, :] += columns_sum(grad_normed)
    sums[2:3, :] += columns_sum(grad_mid)
    sums[3:4, :] += columns_sum(result)
    result = result.astype(BF)
    grad_joined_out[...] = result
    split_halves(ids, dot(result, full[...], (1, 1)).astype(BF), mine, away)


def leave(values, out):
    images = values.shape[0] // PAD
    out[...] = jnp.concatenate([values[i * PAD : i * PAD + SEQ] for i in range(images)], axis=0).astype(out.dtype)


def output_kernel(ids, one, two, mid, out):
    leave(mid[...] + join_halves(ids, one, two), out)


def exit_kernel(ids, one, two, grad_mid, tokens, gain, out, sums):
    grad_normed = join_halves(ids, one, two)
    centred, inverse = normalize(tokens[...].astype(F32))
    leave(grad_mid[...] + norm_back(grad_normed, centred, inverse, gain[...]), out)
    sums[...] = jnp.concatenate([columns_sum(grad_normed * centred), columns_sum(grad_normed)], axis=0)


def run(kernel, ids, args, outs, flops, images=None, scratch=()):
    def spec(shape, how):
        if images is None:
            return pl.BlockSpec(memory_space=pltpu.VMEM)
        if how == 0:
            return pl.BlockSpec(shape, lambda i: (0,) * len(shape))
        return pl.BlockSpec((shape[0] // images, *shape[1:]), lambda i: (i,) + (0,) * (len(shape) - 1))

    in_specs = [spec(a.shape, how) for a, how in args]
    arrays = [a for a, _ in args]
    if ids is not None:
        in_specs = [pl.BlockSpec(memory_space=pltpu.SMEM)] + in_specs
        arrays = [ids] + arrays
    size = sum(a.size * a.dtype.itemsize for a in arrays)
    shapes = [jax.ShapeDtypeStruct(*s) for s, _ in outs]
    size += sum(s.size * s.dtype.itemsize for s in shapes)
    how = {} if images is None else {"grid": (images,)}
    return pl.pallas_call(
        kernel,
        out_shape=shapes,
        in_specs=in_specs,
        out_specs=[spec(s[0], how) for s, how in outs],
        scratch_shapes=list(scratch),
        compiler_params=pltpu.CompilerParams(vmem_limit_bytes=48 * 1024 * 1024),
        cost_estimate=pl.CostEstimate(flops=int(flops), bytes_accessed=int(size), transcendentals=0),
        **how,
    )(*arrays)


def on_device(
    tokens,
    attn_gain,
    attn_shift,
    query_weight,
    key_weight,
    value_weight,
    query_bias,
    value_bias,
    proj_weight,
    proj_bias,
    mlp_gain,
    mlp_shift,
    expand_weight,
    expand_bias,
    shrink_weight,
    shrink_bias,
    cotangent,
):
    grid = Grid()
    ids = grid.ids
    wide = query_weight.shape[1]
    model = tokens.shape[1]
    hidden_here = expand_weight.shape[1]
    images = tokens.shape[0] // SEQ
    rows = images * PAD
    heads = wide // HD
    half = model // 2
    assert heads == 3

    def pack(query, key, value, proj):
        parts = []
        for i, array in enumerate((query, key, value)):
            parts += [array, proj[..., i * HD : (i + 1) * HD]]
        return jnp.concatenate(parts, axis=-1)

    packed = pack(query_weight, key_weight, value_weight, proj_weight.T)
    biases = grid.fetch(jnp.concatenate([query_bias, value_bias, expand_bias]), 0)
    here, there = gather_block(grid, packed)
    e_here, e_there = gather_block(grid, expand_weight, here[1])
    s_here, s_there = gather_block(grid, shrink_weight, e_here[1])
    q_bias, v_bias, e_bias = biases[:wide], biases[wide : 2 * wide], biases[2 * wide :]
    nothing = jnp.zeros_like(q_bias)
    joined_bias = pack(q_bias, nothing, v_bias, nothing)

    def line(vector):
        return vector.reshape(1, -1)

    def spread(bias):
        own = jnp.arange(model) // bias.shape[0] == grid.col
        return line(jnp.where(own, jnp.tile(bias, grid.cols), 0.0))

    tokens_pad, first_in, cot, cot_sum = run(
        enter_kernel,
        None,
        [(tokens, 0), (cotangent, 0), (line(attn_gain), 0), (line(attn_shift), 0)],
        [(((rows, model), BF), 0), (((rows, model), BF), 0), (((rows, model), BF), 0), (((1, model), F32), 0)],
        rows * model * 20,
    )
    halves = [(((rows, half), BF), 1), (((rows, half), BF), 1)]
    full, proj, joined, attended, probs, mine, away = run(
        attend_kernel,
        ids,
        [(first_in, 1)] + [(a, 0) for a in (*here, *there, line(joined_bias), spread(proj_bias))],
        [
            (((model, model), BF), 0),
            (((model, 2 * LANES), BF), 0),
            (((rows, model), BF), 1),
            (((rows, 2 * LANES), BF), 1),
            (((heads * images, PAD, PAD), BF), 1),
        ]
        + halves,
        2 * rows * model * (model + 2 * wide),
        images,
    )
    one, two = sum_cols(grid, mine, away)
    shrink, mid, second_in, hidden, grad_pre, mine, away, pre_sum = run(
        mlp_kernel,
        ids,
        [(tokens_pad, 1), (one, 1), (two, 1), (cot, 1)]
        + [(line(a), 0) for a in (mlp_gain, mlp_shift, e_bias)]
        + [(a, 0) for a in (*e_here, *e_there, *s_here, *s_there)],
        [
            (((model, hidden_here), BF), 0),
            (((rows, model), F32), 1),
            (((rows, model), BF), 1),
            (((rows, hidden_here), BF), 1),
            (((rows, hidden_here), BF), 1),
        ]
        + halves
        + [(((1, hidden_here), F32), 0)],
        2 * rows * model * hidden_here * 3,
        images,
        [pltpu.VMEM((model, hidden_here), BF)],
    )
    one, two = sum_cols(grid, mine, away)

    def pieces(width):
        shape = (grid.cols, model // (2 * grid.cols), width)
        return [((shape, BF), 0), ((shape, BF), 0)]

    def outer(left, right):
        return run(
            outer_kernel,
            ids,
            [(left, 0), (right, 0)],
            pieces(right.shape[1]),
            2 * rows * model * right.shape[1],
            scratch=[pltpu.VMEM((model, right.shape[1]), BF)],
        )

    grad_shrink = reduce_block(grid, *outer(cot, hidden))
    grad_expand = reduce_block(grid, *outer(second_in, grad_pre))
    mine, away = run(
        shrink_kernel,
        ids,
        [(hidden, 1), (shrink, 0), (spread(shrink_bias), 0)],
        halves,
        2 * rows * model * hidden_here,
        images,
    )
    out_one, out_two = sum_cols(grid, mine, away)
    (output,) = run(
        output_kernel,
        ids,
        [(out_one, 0), (out_two, 0), (mid, 0)],
        [((tokens.shape, BF), 0)],
        rows * model,
    )

    grad_mid, grad_mid_b, grad_joined, mine, away, sums = run(
        attend_back_kernel,
        ids,
        [(one, 1), (two, 1), (mid, 1), (cot, 1), (line(mlp_gain), 0), (full, 0), (proj, 0), (joined, 1), (probs, 1)],
        [(((rows, model), F32), 1), (((rows, model), BF), 1), (((rows, model), BF), 1)]
        + halves
        + [(((4, model), F32), 0)],
        2 * rows * model * (model + 2 * wide),
        images,
    )
    packed_pieces = run(
        joined_outer_kernel,
        ids,
        [(first_in, 0), (grad_joined, 0), (grad_mid_b, 0), (attended, 0)],
        pieces(model),
        2 * rows * model * model,
        scratch=[pltpu.VMEM((model, model), BF)],
    )
    one, two = sum_cols(grid, mine, away)
    grad_packed = reduce_block(grid, *packed_pieces)
    grad_tokens, late = run(
        exit_kernel,
        ids,
        [(one, 0), (two, 0), (grad_mid, 0), (tokens_pad, 0), (line(attn_gain), 0)],
        [((tokens.shape, BF), 0), (((2, model), F32), 0)],
        rows * model * 20,
    )
    late = sum_tokens(grid, late)

    step = wide + HD
    blocks = jnp.concatenate([sums[3, :wide], sums[3, 2 * step : 2 * step + wide], pre_sum[0]])
    slots = jnp.where(jnp.arange(grid.rows)[:, None] == grid.block, blocks[None], 0.0)
    early = jnp.concatenate([(sums[:3] / grid.cols).reshape(-1), cot_sum[0] / grid.cols, slots.reshape(-1)])
    early = sum_all(grid, early.reshape(-1, LANES)).reshape(-1)
    whole = early[: 4 * model].reshape(4, model)
    blocks = lax.dynamic_index_in_dim(early[4 * model :].reshape(grid.rows, -1), grid.row, 0, keepdims=False)

    def own_columns(vector):
        width = vector.shape[0] // grid.cols
        return lax.dynamic_slice_in_dim(vector, grid.col * width, width, 0)

    grad_proj = jnp.concatenate([grad_packed[:, i * step + wide : (i + 1) * step] for i in range(3)], axis=1).T
    return (
        output,
        grad_tokens,
        late[0],
        late[1],
        grad_packed[:, :wide],
        grad_packed[:, step : step + wide],
        grad_packed[:, 2 * step : 2 * step + wide],
        blocks[:wide],
        blocks[wide : 2 * wide],
        grad_proj,
        own_columns(whole[2]),
        whole[0],
        whole[1],
        grad_expand,
        blocks[2 * wide :],
        grad_shrink,
        own_columns(whole[3]),
    )


def solution(mesh):
    placed = (
        P(("dp", "row"), None),
        P(),
        P(),
        P("col", "row"),
        P("col", "row"),
        P("col", "row"),
        P("row"),
        P("row"),
        P("row", "col"),
        P("col"),
        P(),
        P(),
        P("col", "row"),
        P("row"),
        P("col", "row"),
        P("col"),
        P(("dp", "row"), None),
    )
    return jax.shard_map(
        on_device,
        mesh=mesh,
        in_specs=placed,
        out_specs=(
            P(("dp", "row"), None),
            P(("dp", "row"), None),
            P(),
            P(),
            P("col", "row"),
            P("col", "row"),
            P("col", "row"),
            P("row"),
            P("row"),
            P("row", "col"),
            P("col"),
            P(),
            P(),
            P("col", "row"),
            P("row"),
            P("col", "row"),
            P("col"),
        ),
        check_vma=False,
    )
```

```python
import jax
import jax.numpy as jnp
from jax import lax
from jax.experimental import pallas as pl
from jax.experimental.pallas import tpu as pltpu
from jax.sharding import PartitionSpec as P

HD = 64
SEQ = 197
PAD = 208
LANES = 128
EPS = 1e-06
BF = jnp.bfloat16
F32 = jnp.float32


def mirrored(index, size):
    out, step = 0, 1
    while step < size:
        out = out * 2 + (index // step) % 2
        step *= 2
    return out


class Grid:
    def __init__(self):
        self.rows = lax.axis_size("row")
        self.cols = lax.axis_size("col")
        self.dps = lax.axis_size("dp")
        assert self.rows == self.cols
        self.row = lax.axis_index("row")
        self.col = lax.axis_index("col")
        self.dp = lax.axis_index("dp")
        self.mirror = [mirrored(c, self.cols) for c in range(self.cols)]
        self.block = self.row ^ jnp.array(self.mirror, jnp.int32)[self.col]
        self.ids = jnp.stack([self.col, self.dp % 2]).astype(jnp.int32)

    def moves(self, base):
        for d in range(self.dps):
            for r in range(self.rows):
                for c in range(self.cols):
                    holder = (d * self.rows + (r ^ self.mirror[c])) * self.cols + (c ^ (base + d % 2))
                    yield (d * self.rows + r) * self.cols + c, holder

    def fetch(self, array, base):
        return lax.ppermute(array, ("dp", "row", "col"), [(holder, me) for me, holder in self.moves(base)])

    def give(self, array, base):
        return lax.ppermute(array, ("dp", "row", "col"), [(me, holder) for me, holder in self.moves(base)])

    def fetch_own(self, array):
        pairs = []
        for r in range(self.rows):
            for c in range(self.cols):
                pairs.append(((r ^ self.mirror[c]) * self.cols + c, r * self.cols + c))
        return lax.ppermute(array, ("row", "col"), pairs)

    def swap(self, array, axis, flip):
        size = lax.axis_size(axis)
        return lax.ppermute(array, axis, [(i, i ^ flip) for i in range(size)])


def after(value, *others):
    return lax.optimization_barrier((value, others))[0]


BASES = (2, 0)


def gather_block(grid, shard, starts=None):
    pieces = []
    for base, start in zip(BASES, starts or (None, None)):
        piece = grid.fetch(shard if start is None else after(shard, start), base)
        pieces += [piece, grid.swap(piece, "dp", 1)]
    return pieces


def finish(grid, parts):
    total = parts[0] + parts[1]
    step = 2
    while step < grid.dps:
        total = total + grid.swap(total, "dp", step)
        step *= 2
    return total.astype(F32) + grid.swap(total, "dp", 1).astype(F32)


def sum_two(grid, mine, away, others=()):
    mine = after(mine + grid.swap(away, "col", 1), *others)
    total, step = mine, 2
    while step < grid.cols:
        total = total + grid.swap(total, "col", step)
        step *= 2
    return mine, total


def sum_all(grid, array):
    for axis in ("col", "row", "dp"):
        step = 1
        while step < lax.axis_size(axis):
            array = array + grid.swap(array, axis, step)
            step *= 2
    return array


def dot(left, right, contract):
    return lax.dot_general(left, right, ((contract[:1], contract[1:]), ((), ())), preferred_element_type=F32)


def normalize(values):
    mean_part = jnp.mean(values, axis=-1, keepdims=True)
    square_part = jnp.mean(values * values, axis=-1, keepdims=True)
    inverse = lax.rsqrt(square_part - mean_part * mean_part + EPS)
    return (values - mean_part) * inverse, inverse


def norm_back(grad_normed, centred, inverse, norm_gain):
    scaled = grad_normed * norm_gain
    first_mean = jnp.mean(scaled, axis=-1, keepdims=True)
    second_mean = jnp.mean(scaled * centred, axis=-1, keepdims=True)
    return inverse * (scaled - first_mean - centred * second_mean)


def gelu_parts(pre_act):
    cdf_value = 0.5 * (1.0 + lax.erf(pre_act * 0.7071067811865476))
    density = jnp.exp(-0.5 * pre_act * pre_act) * 0.3989422804014327
    return (pre_act * cdf_value, cdf_value + pre_act * density)


def columns_sum(values):
    return jnp.sum(values, axis=0, keepdims=True)


def low_lanes(shape):
    return lax.broadcasted_iota(jnp.int32, shape, len(shape) - 1) % LANES < HD


def low(values):
    return jnp.where(low_lanes(values.shape), values, jnp.zeros_like(values))


def high(values):
    return jnp.where(low_lanes(values.shape), jnp.zeros_like(values), values)


def piece_rows(ids, which, size):
    side = ids[1] if which % 2 == 0 else 1 - ids[1]
    return pl.ds(pl.multiple_of((ids[0] ^ (BASES[which // 2] + side)) * size, size), size)


def copies(ids, pieces, full, sems):
    return [
        pltpu.make_async_copy(piece, full.at[piece_rows(ids, i, piece.shape[0])], sems.at[i])
        for i, piece in enumerate(pieces)
    ]


def place(ids, pieces, full, sems):
    for copy in copies(ids, pieces, full, sems):
        copy.start()
    for copy in copies(ids, pieces, full, sems):
        copy.wait()


def split_halves(ids, values, mine, away):
    half = values.shape[1] // 2
    left, right = values[:, :half], values[:, half:]
    first = ids[0] % 2 == 0
    mine[...] = jnp.where(first, left, right)
    away[...] = jnp.where(first, right, left)


def join_halves(ids, mine, other):
    first = ids[0] % 2 == 0
    a, b = mine[...].astype(F32), other[...].astype(F32)
    return jnp.concatenate([jnp.where(first, a, b), jnp.where(first, b, a)], axis=1)


def enter_kernel(tokens, cot, gain, shift, tokens_out, first_out, cot_out, sums):
    images = tokens.shape[0] // SEQ
    total = jnp.zeros((1, tokens.shape[1]), F32)
    for i in range(images):
        blank = jnp.zeros((PAD - SEQ, tokens.shape[1]), F32)
        here = pl.ds(i * PAD, PAD)
        rows = jnp.concatenate([tokens[pl.ds(i * SEQ, SEQ), :].astype(F32), blank], axis=0)
        tokens_out[here, :] = rows.astype(BF)
        centred, _ = normalize(rows)
        first_out[here, :] = (centred * gain[...] + shift[...]).astype(BF)
        rows = jnp.concatenate([cot[pl.ds(i * SEQ, SEQ), :].astype(F32), blank], axis=0)
        cot_out[here, :] = rows.astype(BF)
        total += columns_sum(rows)
    sums[...] = total


def attend_kernel(ids, first, h0, h1, h2, h3, bias, proj_bias, full, proj, joined, attended, probs, mine, away, sems):
    @pl.when(pl.program_id(0) == 0)
    def _():
        place(ids, (h0, h1, h2, h3), full, sems)
        one, two, three = (full[:, i * LANES : (i + 1) * LANES].astype(F32) for i in (1, 3, 5))
        is_low = low_lanes(one.shape)
        proj[:, :LANES] = jnp.where(is_low, pltpu.roll(one, HD, 1), two).astype(BF)
        proj[:, LANES:] = low(pltpu.roll(three, HD, 1)).astype(BF)

    rows = (dot(first[...], full[...], (1, 0)) + bias[...]).astype(BF)
    query = rows[:, : 2 * LANES] * jnp.asarray(HD**-0.5, BF)
    joined[:, : 2 * LANES] = query
    joined[:, 2 * LANES :] = rows[:, 2 * LANES :]
    key, value = rows[:, 2 * LANES : 4 * LANES], rows[:, 4 * LANES :]
    is_key = lax.broadcasted_iota(jnp.int32, (PAD, PAD), 1) < SEQ
    outs = []
    for head in range(3):
        lanes = slice(head // 2 * LANES, (head // 2 + 1) * LANES)
        part = high if head == 1 else low
        scores = dot(query[:, lanes], part(key[:, lanes]), (1, 1))
        scores = jnp.where(is_key, scores, -1e30)
        weights = jnp.exp(scores - jnp.max(scores, axis=-1, keepdims=True))
        weights = (weights * (1.0 / jnp.sum(weights, axis=-1, keepdims=True))).astype(BF)
        probs[head] = weights
        outs.append(dot(weights, part(value[:, lanes]), (1, 0)))
    result = jnp.concatenate([outs[0] + outs[1], outs[2]], axis=1).astype(BF)
    attended[...] = result
    split_halves(ids, (dot(result, proj[...], (1, 1)) + proj_bias[...]).astype(BF), mine, away)


def mlp_kernel(
    ids, tokens, one, two, cot, gain, shift, bias, w0, w1, w2, w3,
    full, mid_out, second_out, hidden_out, pre_out, mine, away, sums, sems
):
    @pl.when(pl.program_id(0) == 0)
    def _():
        for copy in copies(ids, (w0, w1, w2, w3), full, sems):
            copy.start()
        sums[...] = jnp.zeros_like(sums)

    mid = tokens[...].astype(F32) + join_halves(ids, one, two)
    mid_out[...] = mid
    centred, _ = normalize(mid)
    second = (centred * gain[...] + shift[...]).astype(BF)
    second_out[...] = second

    @pl.when(pl.program_id(0) == 0)
    def _():
        for copy in copies(ids, (w0, w1, w2, w3), full, sems):
            copy.wait()

    width = hidden_out.shape[1]
    activ, slope = gelu_parts(dot(second, full[:, :width], (1, 0)) + bias[...])
    hidden_out[...] = activ.astype(BF)
    grad_pre = dot(cot[...], full[:, width:], (1, 0)) * slope
    sums[0:1, :] += columns_sum(grad_pre)
    grad_pre = grad_pre.astype(BF)
    pre_out[...] = grad_pre
    grad_normed = dot(grad_pre, full[:, :width], (1, 1))
    sums[1:2, :] += columns_sum(grad_normed * centred)
    sums[2:3, :] += columns_sum(grad_normed)
    split_halves(ids, grad_normed.astype(BF), mine, away)


def shrink_kernel(ids, hidden, full, bias, mine, away):
    width = hidden.shape[1]
    split_halves(ids, (dot(hidden[...], full[:, width:], (1, 1)) + bias[...]).astype(BF), mine, away)


def deal(ids, full, stay_one, stay_two, away_one, away_two):
    size = stay_one.shape[0]
    for i, ref in enumerate((stay_one, away_one, stay_two, away_two)):
        ref[...] = full[piece_rows(ids, i, size), :]


def outer_kernel(ids, cot, hidden, second, grad_pre, s0, s1, a0, a1, full):
    width = hidden.shape[1]
    full[:, :width] = dot(second[...], grad_pre[...], (0, 0)).astype(BF)
    full[:, width:] = dot(cot[...], hidden[...], (0, 0)).astype(BF)
    deal(ids, full, s0, s1, a0, a1)


def joined_outer_kernel(ids, first, joined, grad_mid, attended, s0, s1, a0, a1, full):
    full[...] = dot(first[...], joined[...], (0, 0)).astype(BF)
    other = dot(grad_mid[...], attended[...], (0, 0))
    turned = (pltpu.roll(other[:, :LANES], HD, 1), other[:, :LANES], pltpu.roll(other[:, LANES:], HD, 1))
    for i, values in enumerate(turned):
        lanes = pl.ds((2 * i + 1) * LANES, LANES)
        is_low = low_lanes(values.shape)
        full[:, lanes] = jnp.where(is_low, full[:, lanes].astype(F32), values).astype(BF)
    deal(ids, full, s0, s1, a0, a1)


def attend_back_kernel(
    ids, one, two, mid, cot, gain, full, proj, joined, probs,
    grad_mid_out, grad_mid_b_out, grad_joined_out, mine, away, sums
):
    @pl.when(pl.program_id(0) == 0)
    def _():
        sums[...] = jnp.zeros_like(sums)

    grad_normed = join_halves(ids, one, two)
    centred, inverse = normalize(mid[...])
    grad_mid = cot[...].astype(F32) + norm_back(grad_normed, centred, inverse, gain[...])
    grad_mid_out[...] = grad_mid
    grad_mid_b = grad_mid.astype(BF)
    grad_mid_b_out[...] = grad_mid_b
    grad_att = dot(grad_mid_b, proj[...], (1, 0)).astype(BF)
    query, key, value = (joined[:, i * 2 * LANES : (i + 1) * 2 * LANES] for i in range(3))
    queries, keys, values = [], [], []
    for head in range(3):
        lanes = slice(head // 2 * LANES, (head // 2 + 1) * LANES)
        part = high if head == 1 else low
        weights = probs[head]
        wide = weights.astype(F32)
        grad_weights = dot(grad_att[:, lanes], part(value[:, lanes]), (1, 1))
        row_delta = jnp.sum(wide * grad_weights, axis=-1, keepdims=True)
        grad_scores = (wide * (grad_weights - row_delta)).astype(BF)
        queries.append(dot(grad_scores, part(key[:, lanes]), (1, 0)))
        keys.append(dot(grad_scores, part(query[:, lanes]), (0, 0)))
        values.append(dot(weights, part(grad_att[:, lanes]), (0, 0)))
    scale = HD**-0.5
    result = jnp.concatenate(
        [(queries[0] + queries[1]) * scale, queries[2] * scale, keys[0] + keys[1], keys[2], values[0] + values[1], values[2]],
        axis=1,
    )
    sums[0:1, :] += columns_sum(grad_mid)
    sums[1:2, :] += columns_sum(result)
    result = result.astype(BF)
    grad_joined_out[...] = result
    split_halves(ids, dot(result, full[...], (1, 1)).astype(BF), mine, away)


def leave(values, out):
    images = values.shape[0] // PAD
    out[...] = jnp.concatenate([values[i * PAD : i * PAD + SEQ] for i in range(images)], axis=0).astype(out.dtype)


def output_kernel(ids, one, two, mid, out):
    leave(mid[...] + join_halves(ids, one, two), out)


def exit_kernel(ids, one, two, grad_mid, tokens, gain, out):
    grad_normed = join_halves(ids, one, two)
    centred, inverse = normalize(tokens[...].astype(F32))
    leave(grad_mid[...] + norm_back(grad_normed, centred, inverse, gain[...]), out)


def sums_kernel(ids, mine, away, tokens, block, cot_sum, mlp_sums, back_sums, out):
    share = 1.0 / ((out.shape[0] - 6) // 2)
    grad_normed = join_halves(ids, mine, away)
    centred, _ = normalize(tokens[...].astype(F32))
    out[...] = jnp.zeros_like(out)
    out[0:1, :] = columns_sum(grad_normed * centred)
    out[1:2, :] = columns_sum(grad_normed)
    out[2:4, :] = mlp_sums[1:3, :]
    out[4:5, :] = back_sums[0:1, :] * share
    out[5:6, :] = cot_sum[...] * share
    out[pl.ds(6 + 2 * block[0], 1), :] = back_sums[1:2, :]
    out[pl.ds(7 + 2 * block[0], 1), :] = mlp_sums[0:1, :]


def run(kernel, ids, args, outs, flops, images=None, scratch=()):
    def spec(shape, how):
        if how == 3:
            return pl.BlockSpec(memory_space=pltpu.SMEM)
        if how == 2:
            return pl.BlockSpec(memory_space=pl.ANY)
        if images is None:
            return pl.BlockSpec(memory_space=pltpu.VMEM)
        if how == 0:
            return pl.BlockSpec(shape, lambda i: (0,) * len(shape))
        return pl.BlockSpec((shape[0] // images, *shape[1:]), lambda i: (i,) + (0,) * (len(shape) - 1))

    in_specs = [spec(a.shape, how) for a, how in args]
    arrays = [a for a, _ in args]
    if ids is not None:
        in_specs = [pl.BlockSpec(memory_space=pltpu.SMEM)] + in_specs
        arrays = [ids] + arrays
    size = sum(a.size * a.dtype.itemsize for a in arrays)
    shapes = [jax.ShapeDtypeStruct(*s) for s, _ in outs]
    size += sum(s.size * s.dtype.itemsize for s in shapes)
    how = {} if images is None else {"grid": (images,)}
    return list(pl.pallas_call(
        kernel,
        out_shape=shapes,
        in_specs=in_specs,
        out_specs=[spec(s[0], how) for s, how in outs],
        scratch_shapes=list(scratch),
        compiler_params=pltpu.CompilerParams(vmem_limit_bytes=60 * 1024 * 1024),
        cost_estimate=pl.CostEstimate(flops=1, bytes_accessed=1, transcendentals=0),
        **how,
    )(*arrays))


def on_device(
    tokens,
    attn_gain,
    attn_shift,
    query_weight,
    key_weight,
    value_weight,
    query_bias,
    value_bias,
    proj_weight,
    proj_bias,
    mlp_gain,
    mlp_shift,
    expand_weight,
    expand_bias,
    shrink_weight,
    shrink_bias,
    cotangent,
):
    grid = Grid()
    ids = grid.ids
    wide = query_weight.shape[1]
    model = tokens.shape[1]
    hidden_here = expand_weight.shape[1]
    images = tokens.shape[0] // SEQ
    rows = images * PAD
    heads = wide // HD
    half = model // 2
    assert heads == 3

    def pack(query, key, value, proj):
        parts = []
        for i, array in enumerate((query, key, value)):
            parts += [array, proj[..., i * HD : (i + 1) * HD]]
        return jnp.concatenate(parts, axis=-1)

    packed = pack(query_weight, key_weight, value_weight, proj_weight.T)
    both = jnp.concatenate([expand_weight, shrink_weight], axis=1)
    biases = grid.fetch_own(jnp.concatenate([query_bias, value_bias, expand_bias]))
    p_pieces = gather_block(grid, packed)
    w_pieces = gather_block(grid, after(both, p_pieces[0], p_pieces[2]))
    p_pieces[0] = after(p_pieces[0], w_pieces[0])
    q_bias, v_bias, e_bias = biases[:wide], biases[wide : 2 * wide], biases[2 * wide :]
    nothing = jnp.zeros_like(q_bias)
    joined_bias = pack(q_bias, nothing, v_bias, nothing)

    def line(vector):
        return vector.reshape(1, -1)

    def spread(bias):
        own = jnp.arange(model) // bias.shape[0] == grid.col
        return line(jnp.where(own, jnp.tile(bias, grid.cols), 0.0))

    tokens_pad, first_in, cot, cot_sum = run(
        enter_kernel,
        None,
        [(tokens, 0), (cotangent, 0), (line(attn_gain), 0), (line(attn_shift), 0)],
        [(((rows, model), BF), 0), (((rows, model), BF), 0), (((rows, model), BF), 0), (((1, model), F32), 0)],
        rows * model * 20,
    )
    halves = [(((rows, half), BF), 1), (((rows, half), BF), 1)]
    full, proj, joined, attended, probs, mine, away = run(
        attend_kernel,
        ids,
        [(first_in, 1)] + [(a, 2) for a in p_pieces] + [(line(joined_bias), 0), (spread(proj_bias), 0)],
        [
            (((model, model), BF), 0),
            (((model, 2 * LANES), BF), 0),
            (((rows, model), BF), 1),
            (((rows, 2 * LANES), BF), 1),
            (((heads * images, PAD, PAD), BF), 1),
        ]
        + halves,
        2 * rows * model * (model + 2 * wide),
        images,
        [pltpu.SemaphoreType.DMA((4,))],
    )
    _, one = sum_two(grid, mine, away, (w_pieces[1], w_pieces[2]))
    two = grid.swap(after(one, w_pieces[3]), "col", 1)
    wide_full, mid, second_in, hidden, grad_pre, mine, away, mlp_sums = run(
        mlp_kernel,
        ids,
        [(tokens_pad, 1), (one, 1), (two, 1), (cot, 1)]
        + [(line(a), 0) for a in (mlp_gain, mlp_shift, e_bias)]
        + [(a, 2) for a in w_pieces],
        [
            (((model, 2 * hidden_here), BF), 0),
            (((rows, model), F32), 1),
            (((rows, model), BF), 1),
            (((rows, hidden_here), BF), 1),
            (((rows, hidden_here), BF), 1),
        ]
        + halves
        + [(((3, hidden_here), F32), 0)],
        2 * rows * model * hidden_here * 3,
        images,
        [pltpu.SemaphoreType.DMA((4,))],
    )

    def pieces(width):
        return [(((model // grid.cols, width), BF), 0)] * 4

    mine, one = sum_two(grid, mine, away)
    hidden = after(hidden, mine)
    parts = run(
        outer_kernel,
        ids,
        [(cot, 0), (hidden, 0), (second_in, 0), (grad_pre, 0)],
        pieces(2 * hidden_here),
        4 * rows * model * hidden_here,
        scratch=[pltpu.VMEM((model, 2 * hidden_here), BF)],
    )
    got = [grid.swap(a, "dp", 1) for a in parts[2:]]
    mine_out, away_out = run(
        shrink_kernel,
        ids,
        [(after(hidden, parts[0]), 1), (wide_full, 0), (spread(shrink_bias), 0)],
        halves,
        2 * rows * model * hidden_here,
        images,
    )
    mine_out, out_one = sum_two(grid, mine_out, away_out)
    one = after(one, away_out)
    two = grid.swap(one, "col", 1)

    grad_mid, grad_mid_b, grad_joined, mine, away, back_sums = run(
        attend_back_kernel,
        ids,
        [(one, 1), (two, 1), (mid, 1), (cot, 1), (line(mlp_gain), 0), (full, 0), (proj, 0), (joined, 1), (probs, 1)],
        [(((rows, model), F32), 1), (((rows, model), BF), 1), (((rows, model), BF), 1)]
        + halves
        + [(((2, model), F32), 0)],
        2 * rows * model * (model + 2 * wide),
        images,
    )
    packed_parts = run(
        joined_outer_kernel,
        ids,
        [(first_in, 0), (grad_joined, 0), (grad_mid_b, 0), (attended, 0)],
        pieces(model),
        2 * rows * model * model,
        scratch=[pltpu.VMEM((model, model), BF)],
    )
    packed_got = [grid.swap(a, "dp", 1) for a in packed_parts[2:]]
    partial, away_here = mine, away
    away = after(away, packed_parts[0], out_one)
    mine, one = sum_two(grid, mine, away)
    parts = after(parts, mine)
    pairs = [parts[i] + got[i] for i in range(2)]
    later = grid.give(pairs[1], BASES[1])
    assert hidden_here == model
    (totals,) = run(
        sums_kernel,
        ids,
        [(after(partial, pairs[0]), 0), (away_here, 0), (tokens_pad, 0)]
        + [(grid.block.reshape(1).astype(jnp.int32), 3), (cot_sum, 0), (mlp_sums, 0), (back_sums, 0)],
        [(((6 + 2 * grid.rows, model), F32), 0)],
        rows * model * 10,
    )
    totals = sum_all(grid, totals)
    packed_pairs = [packed_parts[i] + packed_got[i] for i in range(2)]
    two = grid.swap(one, "col", 1)
    pairs[0] = after(pairs[0], one)
    sooner = grid.give(pairs[0], BASES[0])
    grad_packed = finish(grid, [grid.give(pair, base) for pair, base in zip(packed_pairs, BASES)])
    (grad_tokens,) = run(
        exit_kernel,
        ids,
        [(one, 0), (two, 0), (grad_mid, 0), (tokens_pad, 0), (line(attn_gain), 0)],
        [((tokens.shape, BF), 0)],
        rows * model * 20,
    )
    (output,) = run(
        output_kernel,
        ids,
        [(out_one, 0), (grid.swap(out_one, "col", 1), 0), (mid, 0)],
        [((tokens.shape, BF), 0)],
        rows * model,
    )
    grad_both = finish(grid, [sooner, later])
    step = wide + HD
    blocks = lax.dynamic_slice_in_dim(totals, 6 + 2 * grid.row, 2, 0)

    def own_columns(vector):
        width = vector.shape[0] // grid.cols
        return lax.dynamic_slice_in_dim(vector, grid.col * width, width, 0)

    grad_proj = jnp.concatenate([grad_packed[:, i * step + wide : (i + 1) * step] for i in range(3)], axis=1).T
    return (
        output,
        grad_tokens,
        totals[0],
        totals[1],
        grad_packed[:, :wide],
        grad_packed[:, step : step + wide],
        grad_packed[:, 2 * step : 2 * step + wide],
        blocks[0, :wide],
        blocks[0, 2 * step : 2 * step + wide],
        grad_proj,
        own_columns(totals[4]),
        totals[2],
        totals[3],
        grad_both[:, :hidden_here],
        blocks[1],
        grad_both[:, hidden_here:],
        own_columns(totals[5]),
    )


def solution(mesh):
    placed = (
        P(("dp", "row"), None),
        P(),
        P(),
        P("col", "row"),
        P("col", "row"),
        P("col", "row"),
        P("row"),
        P("row"),
        P("row", "col"),
        P("col"),
        P(),
        P(),
        P("col", "row"),
        P("row"),
        P("col", "row"),
        P("col"),
        P(("dp", "row"), None),
    )
    return jax.shard_map(
        on_device,
        mesh=mesh,
        in_specs=placed,
        out_specs=(
            P(("dp", "row"), None),
            P(("dp", "row"), None),
            P(),
            P(),
            P("col", "row"),
            P("col", "row"),
            P("col", "row"),
            P("row"),
            P("row"),
            P("row", "col"),
            P("col"),
            P(),
            P(),
            P("col", "row"),
            P("row"),
            P("col", "row"),
            P("col"),
        ),
        check_vma=False,
    )
```

```python
import jax
import jax.numpy as jnp
from jax import lax
from jax.experimental import pallas as pl
from jax.experimental.pallas import tpu as pltpu
from jax.sharding import PartitionSpec as P

HD = 64
SEQ = 197
PAD = 208
LANES = 128
SUMS = 16
CUT = 320
EPS = 1e-06
BF = jnp.bfloat16
F32 = jnp.float32


def mirrored(index, size):
    out, step = 0, 1
    while step < size:
        out = out * 2 + (index // step) % 2
        step *= 2
    return out


class Grid:
    def __init__(self):
        self.rows = lax.axis_size("row")
        self.cols = lax.axis_size("col")
        self.dps = lax.axis_size("dp")
        assert self.rows == self.cols
        self.row = lax.axis_index("row")
        self.col = lax.axis_index("col")
        self.dp = lax.axis_index("dp")
        self.mirror = [mirrored(c, self.cols) for c in range(self.cols)]
        self.block = self.row ^ jnp.array(self.mirror, jnp.int32)[self.col]
        self.ids = jnp.stack([self.col, self.dp % 2]).astype(jnp.int32)

    def moves(self, base):
        for d in range(self.dps):
            for r in range(self.rows):
                for c in range(self.cols):
                    holder = (d * self.rows + (r ^ self.mirror[c])) * self.cols + (c ^ (base + d % 2))
                    yield (d * self.rows + r) * self.cols + c, holder

    def fetch(self, array, base):
        return lax.ppermute(array, ("dp", "row", "col"), [(holder, me) for me, holder in self.moves(base)])

    def give(self, array, base):
        return lax.ppermute(array, ("dp", "row", "col"), [(me, holder) for me, holder in self.moves(base)])

    def fetch_own(self, array):
        pairs = []
        for r in range(self.rows):
            for c in range(self.cols):
                pairs.append(((r ^ self.mirror[c]) * self.cols + c, r * self.cols + c))
        return lax.ppermute(array, ("row", "col"), pairs)

    def swap(self, array, axis, flip):
        size = lax.axis_size(axis)
        return lax.ppermute(array, axis, [(i, i ^ flip) for i in range(size)])


def after(value, *others):
    return lax.optimization_barrier((value, others))[0]


BASES = (2, 0)


def gather_block(grid, shard, starts=None):
    pieces = []
    for base, start in zip(BASES, starts or (None, None)):
        piece = grid.fetch(shard if start is None else after(shard, start), base)
        pieces += [piece, grid.swap(piece, "dp", 1)]
    return pieces


def finish(grid, total):
    step = 2
    while step < grid.dps:
        total = total + grid.swap(total, "dp", step)
        step *= 2
    return total.astype(F32) + grid.swap(total, "dp", 1).astype(F32)


def sum_two(grid, mine, away, others=()):
    mine = after(mine + grid.swap(away, "col", 1), *others)
    total, step = mine, 2
    while step < grid.cols:
        total = total + grid.swap(total, "col", step)
        step *= 2
    return mine, total


def sum_axis(grid, array, axis, step):
    while step < lax.axis_size(axis):
        array = array + grid.swap(array, axis, step)
        step *= 2
    return array


def dot(left, right, contract):
    return lax.dot_general(left, right, ((contract[:1], contract[1:]), ((), ())), preferred_element_type=F32)


def normalize(values):
    mean_part = jnp.mean(values, axis=-1, keepdims=True)
    square_part = jnp.mean(values * values, axis=-1, keepdims=True)
    inverse = lax.rsqrt(square_part - mean_part * mean_part + EPS)
    return (values - mean_part) * inverse, inverse


def norm_back(grad_normed, centred, inverse, norm_gain):
    scaled = grad_normed * norm_gain
    first_mean = jnp.mean(scaled, axis=-1, keepdims=True)
    second_mean = jnp.mean(scaled * centred, axis=-1, keepdims=True)
    return inverse * (scaled - first_mean - centred * second_mean)


def gelu_parts(pre_act):
    cdf_value = 0.5 * (1.0 + lax.erf(pre_act * 0.7071067811865476))
    density = jnp.exp(-0.5 * pre_act * pre_act) * 0.3989422804014327
    return (pre_act * cdf_value, cdf_value + pre_act * density)


def columns_sum(values):
    return jnp.sum(values, axis=0, keepdims=True)


def low_lanes(shape):
    return lax.broadcasted_iota(jnp.int32, shape, len(shape) - 1) % LANES < HD


def low(values):
    return jnp.where(low_lanes(values.shape), values, jnp.zeros_like(values))


def high(values):
    return jnp.where(low_lanes(values.shape), jnp.zeros_like(values), values)


def piece_rows(ids, which, size):
    side = ids[1] if which % 2 == 0 else 1 - ids[1]
    return pl.ds(pl.multiple_of((ids[0] ^ (BASES[which // 2] + side)) * size, size), size)


def copies(ids, pieces, full, sems):
    return [
        pltpu.make_async_copy(piece, full.at[piece_rows(ids, i, piece.shape[0])], sems.at[i])
        for i, piece in enumerate(pieces)
    ]


def place(ids, pieces, full, sems):
    for copy in copies(ids, pieces, full, sems):
        copy.start()
    for copy in copies(ids, pieces, full, sems):
        copy.wait()


def split_halves(ids, values, mine, away):
    half = values.shape[1] // 2
    left, right = values[:, :half], values[:, half:]
    first = ids[0] % 2 == 0
    mine[...] = jnp.where(first, left, right)
    away[...] = jnp.where(first, right, left)


def join_halves(ids, mine, other):
    first = ids[0] % 2 == 0
    a, b = mine[...].astype(F32), other[...].astype(F32)
    return jnp.concatenate([jnp.where(first, a, b), jnp.where(first, b, a)], axis=1)


def enter_kernel(tokens, cot, gain, shift, tokens_out, first_out, cot_out, sums):
    images = tokens.shape[0] // SEQ
    total = jnp.zeros((1, tokens.shape[1]), F32)
    for i in range(images):
        blank = jnp.zeros((PAD - SEQ, tokens.shape[1]), F32)
        here = pl.ds(i * PAD, PAD)
        rows = jnp.concatenate([tokens[pl.ds(i * SEQ, SEQ), :].astype(F32), blank], axis=0)
        tokens_out[here, :] = rows.astype(BF)
        centred, _ = normalize(rows)
        first_out[here, :] = (centred * gain[...] + shift[...]).astype(BF)
        rows = jnp.concatenate([cot[pl.ds(i * SEQ, SEQ), :].astype(F32), blank], axis=0)
        cot_out[here, :] = rows.astype(BF)
        total += columns_sum(rows)
    sums[...] = total


def attend_kernel(ids, first, h0, h1, h2, h3, bias, proj_bias, full, proj, joined, attended, probs, mine, away, sems):
    @pl.when(pl.program_id(0) == 0)
    def _():
        place(ids, (h0, h1, h2, h3), full, sems)
        one, two, three = (full[:, i * LANES : (i + 1) * LANES].astype(F32) for i in (1, 3, 5))
        is_low = low_lanes(one.shape)
        proj[:, :LANES] = jnp.where(is_low, pltpu.roll(one, HD, 1), two).astype(BF)
        proj[:, LANES:] = low(pltpu.roll(three, HD, 1)).astype(BF)

    rows = (dot(first[...], full[...], (1, 0)) + bias[...]).astype(BF)
    query = rows[:, : 2 * LANES] * jnp.asarray(HD**-0.5, BF)
    joined[:, : 2 * LANES] = query
    joined[:, 2 * LANES :] = rows[:, 2 * LANES :]
    key, value = rows[:, 2 * LANES : 4 * LANES], rows[:, 4 * LANES :]
    is_key = lax.broadcasted_iota(jnp.int32, (PAD, PAD), 1) < SEQ
    outs = []
    for head in range(3):
        lanes = slice(head // 2 * LANES, (head // 2 + 1) * LANES)
        part = high if head == 1 else low
        scores = dot(query[:, lanes], part(key[:, lanes]), (1, 1))
        scores = jnp.where(is_key, scores, -1e30)
        weights = jnp.exp(scores - jnp.max(scores, axis=-1, keepdims=True))
        weights = (weights * (1.0 / jnp.sum(weights, axis=-1, keepdims=True))).astype(BF)
        probs[head] = weights
        outs.append(dot(weights, part(value[:, lanes]), (1, 0)))
    result = jnp.concatenate([outs[0] + outs[1], outs[2]], axis=1).astype(BF)
    attended[...] = result
    split_halves(ids, (dot(result, proj[...], (1, 1)) + proj_bias[...]).astype(BF), mine, away)


def mlp_kernel(
    ids, tokens, one, two, cot, gain, shift, bias, w0, w1, w2, w3,
    full, mid_out, second_out, hidden_out, pre_out, mine, away, sums, sems
):
    @pl.when(pl.program_id(0) == 0)
    def _():
        for copy in copies(ids, (w0, w1, w2, w3), full, sems):
            copy.start()
        sums[...] = jnp.zeros_like(sums)

    mid = tokens[...].astype(F32) + join_halves(ids, one, two)
    mid_out[...] = mid
    centred, _ = normalize(mid)
    second = (centred * gain[...] + shift[...]).astype(BF)
    second_out[...] = second

    @pl.when(pl.program_id(0) == 0)
    def _():
        for copy in copies(ids, (w0, w1, w2, w3), full, sems):
            copy.wait()

    width = hidden_out.shape[1]
    activ, slope = gelu_parts(dot(second, full[:, :width], (1, 0)) + bias[...])
    hidden_out[...] = activ.astype(BF)
    grad_pre = dot(cot[...], full[:, width:], (1, 0)) * slope
    sums[...] += columns_sum(grad_pre)
    grad_pre = grad_pre.astype(BF)
    pre_out[...] = grad_pre
    split_halves(ids, dot(grad_pre, full[:, :width], (1, 1)).astype(BF), mine, away)


def shrink_kernel(ids, hidden, full, bias, mine, away):
    width = hidden.shape[1]
    split_halves(ids, (dot(hidden[...], full[:, width:], (1, 1)) + bias[...]).astype(BF), mine, away)


def deal(ids, full, stay_one, stay_two, away_one, away_two):
    size = stay_one.shape[0]
    for i, ref in enumerate((stay_one, away_one, stay_two, away_two)):
        ref[...] = full[piece_rows(ids, i, size), :]


def outer_kernel(ids, cot, hidden, second, grad_pre, s0, s1, a0, a1, full):
    width = hidden.shape[1]
    full[:, :width] = dot(second[...], grad_pre[...], (0, 0)).astype(BF)
    full[:, width:] = dot(cot[...], hidden[...], (0, 0)).astype(BF)
    deal(ids, full, s0, s1, a0, a1)


def joined_outer_kernel(ids, first, joined, grad_mid, attended, sums, pre_sum, cot_sum, s0, s1, away, full):
    full[...] = dot(first[...], joined[...], (0, 0)).astype(BF)
    other = dot(grad_mid[...], attended[...], (0, 0))
    turned = (pltpu.roll(other[:, :LANES], HD, 1), other[:, :LANES], pltpu.roll(other[:, LANES:], HD, 1))
    for i, values in enumerate(turned):
        lanes = pl.ds((2 * i + 1) * LANES, LANES)
        is_low = low_lanes(values.shape)
        full[:, lanes] = jnp.where(is_low, full[:, lanes].astype(F32), values).astype(BF)
    size = s0.shape[0] - SUMS
    blank = jnp.zeros((SUMS - 6, full.shape[1]), F32)
    below = jnp.concatenate([sums[...], pre_sum[...], cot_sum[...], blank], axis=0).astype(BF)
    places = (s0, s1, away.at[pl.ds(0, size + SUMS)], away.at[pl.ds(size + SUMS, size + SUMS)])
    deal(ids, full, *(ref.at[pl.ds(0, size)] for ref in places))
    for ref in places:
        ref[pl.ds(size, SUMS), :] = below


def attend_back_kernel(
    ids, one, two, mid, cot, gain, full, proj, joined, probs,
    grad_mid_out, grad_mid_b_out, grad_joined_out, mine, away, sums
):
    @pl.when(pl.program_id(0) == 0)
    def _():
        sums[...] = jnp.zeros_like(sums)

    grad_normed = join_halves(ids, one, two)
    centred, inverse = normalize(mid[...])
    grad_mid = cot[...].astype(F32) + norm_back(grad_normed, centred, inverse, gain[...])
    grad_mid_out[...] = grad_mid
    grad_mid_b = grad_mid.astype(BF)
    grad_mid_b_out[...] = grad_mid_b
    grad_att = dot(grad_mid_b, proj[...], (1, 0)).astype(BF)
    query, key, value = (joined[:, i * 2 * LANES : (i + 1) * 2 * LANES] for i in range(3))
    queries, keys, values = [], [], []
    for head in range(3):
        lanes = slice(head // 2 * LANES, (head // 2 + 1) * LANES)
        part = high if head == 1 else low
        weights = probs[head]
        wide = weights.astype(F32)
        grad_weights = dot(grad_att[:, lanes], part(value[:, lanes]), (1, 1))
        row_delta = jnp.sum(wide * grad_weights, axis=-1, keepdims=True)
        grad_scores = (wide * (grad_weights - row_delta)).astype(BF)
        queries.append(dot(grad_scores, part(key[:, lanes]), (1, 0)))
        keys.append(dot(grad_scores, part(query[:, lanes]), (0, 0)))
        values.append(dot(weights, part(grad_att[:, lanes]), (0, 0)))
    scale = HD**-0.5
    result = jnp.concatenate(
        [(queries[0] + queries[1]) * scale, queries[2] * scale, keys[0] + keys[1], keys[2], values[0] + values[1], values[2]],
        axis=1,
    )
    for i, values in enumerate((grad_normed * centred, grad_normed, grad_mid, result)):
        sums[i : i + 1, :] += columns_sum(values)
    result = result.astype(BF)
    grad_joined_out[...] = result
    split_halves(ids, dot(result, full[...], (1, 1)).astype(BF), mine, away)


def leave(values, out):
    images = values.shape[0] // PAD
    out[...] = jnp.concatenate([values[i * PAD : i * PAD + SEQ] for i in range(images)], axis=0).astype(out.dtype)


def output_kernel(ids, one, two, mid, out):
    leave(mid[...] + join_halves(ids, one, two), out)


def exit_kernel(ids, one, upper, lower, grad_mid, tokens, gain, out, sums):
    two = jnp.concatenate([upper[...].astype(F32), lower[...].astype(F32)], axis=0)
    grad_normed = join_halves(ids, one, two)
    centred, inverse = normalize(tokens[...].astype(F32))
    leave(grad_mid[...] + norm_back(grad_normed, centred, inverse, gain[...]), out)
    sums[...] = jnp.concatenate([columns_sum(grad_normed * centred), columns_sum(grad_normed)], axis=0)


def run(kernel, ids, args, outs, flops, images=None, scratch=()):
    def spec(shape, how):
        if how == 3:
            return pl.BlockSpec(memory_space=pltpu.SMEM)
        if how == 2:
            return pl.BlockSpec(memory_space=pl.ANY)
        if images is None:
            return pl.BlockSpec(memory_space=pltpu.VMEM)
        if how == 0:
            return pl.BlockSpec(shape, lambda i: (0,) * len(shape))
        return pl.BlockSpec((shape[0] // images, *shape[1:]), lambda i: (i,) + (0,) * (len(shape) - 1))

    in_specs = [spec(a.shape, how) for a, how in args]
    arrays = [a for a, _ in args]
    if ids is not None:
        in_specs = [pl.BlockSpec(memory_space=pltpu.SMEM)] + in_specs
        arrays = [ids] + arrays
    size = sum(a.size * a.dtype.itemsize for a in arrays)
    shapes = [jax.ShapeDtypeStruct(*s) for s, _ in outs]
    size += sum(s.size * s.dtype.itemsize for s in shapes)
    how = {} if images is None else {"grid": (images,)}
    return list(pl.pallas_call(
        kernel,
        out_shape=shapes,
        in_specs=in_specs,
        out_specs=[spec(s[0], how) for s, how in outs],
        scratch_shapes=list(scratch),
        compiler_params=pltpu.CompilerParams(vmem_limit_bytes=60 * 1024 * 1024),
        cost_estimate=pl.CostEstimate(flops=1, bytes_accessed=1, transcendentals=0),
        **how,
    )(*arrays))


def on_device(
    tokens,
    attn_gain,
    attn_shift,
    query_weight,
    key_weight,
    value_weight,
    query_bias,
    value_bias,
    proj_weight,
    proj_bias,
    mlp_gain,
    mlp_shift,
    expand_weight,
    expand_bias,
    shrink_weight,
    shrink_bias,
    cotangent,
):
    grid = Grid()
    ids = grid.ids
    wide = query_weight.shape[1]
    model = tokens.shape[1]
    hidden_here = expand_weight.shape[1]
    images = tokens.shape[0] // SEQ
    rows = images * PAD
    heads = wide // HD
    half = model // 2
    assert heads == 3

    def pack(query, key, value, proj):
        parts = []
        for i, array in enumerate((query, key, value)):
            parts += [array, proj[..., i * HD : (i + 1) * HD]]
        return jnp.concatenate(parts, axis=-1)

    packed = pack(query_weight, key_weight, value_weight, proj_weight.T)
    both = jnp.concatenate([expand_weight, shrink_weight], axis=1)
    biases = grid.fetch_own(jnp.concatenate([query_bias, value_bias, expand_bias]))
    p_pieces = gather_block(grid, packed)
    w_pieces = gather_block(grid, after(both, p_pieces[0], p_pieces[2]))
    p_pieces[0] = after(p_pieces[0], w_pieces[0])
    q_bias, v_bias, e_bias = biases[:wide], biases[wide : 2 * wide], biases[2 * wide :]
    nothing = jnp.zeros_like(q_bias)
    joined_bias = pack(q_bias, nothing, v_bias, nothing)

    def line(vector):
        return vector.reshape(1, -1)

    def spread(bias):
        own = jnp.arange(model) // bias.shape[0] == grid.col
        return line(jnp.where(own, jnp.tile(bias, grid.cols), 0.0))

    tokens_pad, first_in, cot, cot_sum = run(
        enter_kernel,
        None,
        [(tokens, 0), (cotangent, 0), (line(attn_gain), 0), (line(attn_shift), 0)],
        [(((rows, model), BF), 0), (((rows, model), BF), 0), (((rows, model), BF), 0), (((1, model), F32), 0)],
        rows * model * 20,
    )
    halves = [(((rows, half), BF), 1), (((rows, half), BF), 1)]
    full, proj, joined, attended, probs, mine, away = run(
        attend_kernel,
        ids,
        [(first_in, 1)] + [(a, 2) for a in p_pieces] + [(line(joined_bias), 0), (spread(proj_bias), 0)],
        [
            (((model, model), BF), 0),
            (((model, 2 * LANES), BF), 0),
            (((rows, model), BF), 1),
            (((rows, 2 * LANES), BF), 1),
            (((heads * images, PAD, PAD), BF), 1),
        ]
        + halves,
        2 * rows * model * (model + 2 * wide),
        images,
        [pltpu.SemaphoreType.DMA((4,))],
    )
    _, one = sum_two(grid, mine, away, (w_pieces[1], w_pieces[2]))
    two = grid.swap(after(one, w_pieces[3]), "col", 1)
    wide_full, mid, second_in, hidden, grad_pre, mine, away, mlp_sums = run(
        mlp_kernel,
        ids,
        [(tokens_pad, 1), (one, 1), (two, 1), (cot, 1)]
        + [(line(a), 0) for a in (mlp_gain, mlp_shift, e_bias)]
        + [(a, 2) for a in w_pieces],
        [
            (((model, 2 * hidden_here), BF), 0),
            (((rows, model), F32), 1),
            (((rows, model), BF), 1),
            (((rows, hidden_here), BF), 1),
            (((rows, hidden_here), BF), 1),
        ]
        + halves
        + [(((1, hidden_here), F32), 0)],
        2 * rows * model * hidden_here * 3,
        images,
        [pltpu.SemaphoreType.DMA((4,))],
    )

    def pieces(width, more=0):
        return [(((model // grid.cols + more, width), BF), 0)] * 4

    mine, one = sum_two(grid, mine, away)
    hidden = after(hidden, mine)
    parts = run(
        outer_kernel,
        ids,
        [(cot, 0), (hidden, 0), (second_in, 0), (grad_pre, 0)],
        pieces(2 * hidden_here),
        4 * rows * model * hidden_here,
        scratch=[pltpu.VMEM((model, 2 * hidden_here), BF)],
    )
    got = [grid.swap(a, "dp", 1) for a in parts[2:]]
    one = after(one, parts[0])
    two = grid.swap(one, "col", 1)

    grad_mid, grad_mid_b, grad_joined, mine, away, back_sums = run(
        attend_back_kernel,
        ids,
        [(one, 1), (two, 1), (mid, 1), (cot, 1), (line(mlp_gain), 0), (full, 0), (proj, 0), (joined, 1), (probs, 1)],
        [(((rows, model), F32), 1), (((rows, model), BF), 1), (((rows, model), BF), 1)]
        + halves
        + [(((4, model), F32), 0)],
        2 * rows * model * (model + 2 * wide),
        images,
    )
    sooner = after(parts[0], grad_joined) + got[0]
    packed_parts = run(
        joined_outer_kernel,
        ids,
        [(first_in, 0), (grad_joined, 0), (grad_mid_b, 0), (attended, 0)]
        + [(back_sums, 0), (mlp_sums, 0), (cot_sum, 0)],
        pieces(model, SUMS)[:2] + [(((2 * (model // grid.cols + SUMS), model), BF), 0)],
        2 * rows * model * model,
        scratch=[pltpu.VMEM((model, model), BF)],
    )
    packed_got = grid.swap(packed_parts[2], "dp", 1)
    packed_got = packed_got[: model // grid.cols + SUMS], packed_got[model // grid.cols + SUMS :]
    mine_out, away_out = run(
        shrink_kernel,
        ids,
        [(after(hidden, packed_parts[0]), 1), (wide_full, 0), (spread(shrink_bias), 0)],
        halves,
        2 * rows * model * hidden_here,
        images,
    )
    later = after(parts[1], packed_parts[0]) + got[1]
    away = after(away, packed_parts[0], later, away_out)
    sooner, later = grid.give(sooner, BASES[0]), grid.give(later, BASES[1])
    mine, one = sum_two(grid, mine, away)
    _, out_one = sum_two(grid, mine_out, after(away_out, mine))
    packed_one = after(packed_parts[0], mine, sooner) + packed_got[0]
    packed_two = after(packed_parts[1], packed_one) + packed_got[1]
    packed_given = [grid.give(packed_one, BASES[0]), grid.give(packed_two, BASES[1])]
    total = after(sooner, packed_two, one) + later
    one = after(one, total)
    grad_tokens, late = run(
        exit_kernel,
        ids,
        [(after(one, packed_two), 0)]
        + [(grid.swap(part, "col", 1), 0) for part in (one[:CUT], one[CUT:])]
        + [(grad_mid, 0), (tokens_pad, 0), (line(attn_gain), 0)],
        [((tokens.shape, BF), 0), (((2, model), F32), 0)],
        rows * model * 20,
    )
    grad_both = finish(grid, total)
    packed_total = after(packed_given[0], grad_both, grad_tokens) + packed_given[1]
    (output,) = run(
        output_kernel,
        ids,
        [(after(out_one, packed_total), 0), (grid.swap(out_one, "col", 1), 0), (mid, 0)],
        [((tokens.shape, BF), 0)],
        rows * model,
    )
    grad_packed = finish(grid, packed_total)
    late = sum((grid.swap(late, "row", flip) for flip in range(1, grid.rows)), late)
    late = sum_axis(grid, after(late, grad_both, output), "dp", 1)
    whole, grad_packed = grad_packed[model // grid.cols :], grad_packed[: model // grid.cols]
    step = wide + HD

    def own_columns(vector):
        width = vector.shape[0] // grid.cols
        return lax.dynamic_slice_in_dim(vector, grid.col * width, width, 0)

    grad_proj = jnp.concatenate([grad_packed[:, i * step + wide : (i + 1) * step] for i in range(3)], axis=1).T
    return (
        output,
        grad_tokens,
        late[0],
        late[1],
        grad_packed[:, :wide],
        grad_packed[:, step : step + wide],
        grad_packed[:, 2 * step : 2 * step + wide],
        whole[3, :wide],
        whole[3, 2 * step : 2 * step + wide],
        grad_proj,
        own_columns(whole[2]),
        whole[0],
        whole[1],
        grad_both[:, :hidden_here],
        whole[4],
        grad_both[:, hidden_here:],
        own_columns(whole[5]),
    )


def solution(mesh):
    placed = (
        P(("dp", "row"), None),
        P(),
        P(),
        P("col", "row"),
        P("col", "row"),
        P("col", "row"),
        P("row"),
        P("row"),
        P("row", "col"),
        P("col"),
        P(),
        P(),
        P("col", "row"),
        P("row"),
        P("col", "row"),
        P("col"),
        P(("dp", "row"), None),
    )
    return jax.shard_map(
        on_device,
        mesh=mesh,
        in_specs=placed,
        out_specs=(
            P(("dp", "row"), None),
            P(("dp", "row"), None),
            P(),
            P(),
            P("col", "row"),
            P("col", "row"),
            P("col", "row"),
            P("row"),
            P("row"),
            P("row", "col"),
            P("col"),
            P(),
            P(),
            P("col", "row"),
            P("row"),
            P("col", "row"),
            P("col"),
        ),
        check_vma=False,
    )
```

```python
import jax
import jax.numpy as jnp
from jax import lax
from jax.experimental import pallas as pl
from jax.experimental.pallas import tpu as pltpu
from jax.sharding import PartitionSpec as P

HD = 64
SEQ = 197
PAD = 208
LANES = 128
SUMS = 16
CUT = 320
EPS = 1e-06
BF = jnp.bfloat16
F32 = jnp.float32


def mirrored(index, size):
    out, step = 0, 1
    while step < size:
        out = out * 2 + (index // step) % 2
        step *= 2
    return out


class Grid:
    def __init__(self):
        self.rows = lax.axis_size("row")
        self.cols = lax.axis_size("col")
        self.dps = lax.axis_size("dp")
        assert self.rows == self.cols
        self.row = lax.axis_index("row")
        self.col = lax.axis_index("col")
        self.dp = lax.axis_index("dp")
        self.mirror = [mirrored(c, self.cols) for c in range(self.cols)]
        self.block = self.row ^ jnp.array(self.mirror, jnp.int32)[self.col]
        self.ids = jnp.stack([self.col, self.dp % 2]).astype(jnp.int32)

    def moves(self, base):
        for d in range(self.dps):
            for r in range(self.rows):
                for c in range(self.cols):
                    holder = (d * self.rows + (r ^ self.mirror[c])) * self.cols + (c ^ (base + d % 2))
                    yield (d * self.rows + r) * self.cols + c, holder

    def fetch(self, array, base):
        return lax.ppermute(array, ("dp", "row", "col"), [(holder, me) for me, holder in self.moves(base)])

    def give(self, array, base):
        return lax.ppermute(array, ("dp", "row", "col"), [(me, holder) for me, holder in self.moves(base)])

    def fetch_own(self, array):
        pairs = []
        for r in range(self.rows):
            for c in range(self.cols):
                pairs.append(((r ^ self.mirror[c]) * self.cols + c, r * self.cols + c))
        return lax.ppermute(array, ("row", "col"), pairs)

    def swap(self, array, axis, flip):
        size = lax.axis_size(axis)
        return lax.ppermute(array, axis, [(i, i ^ flip) for i in range(size)])


def after(value, *others):
    return lax.optimization_barrier((value, others))[0]


BASES = (2, 0)


def gather_block(grid, shard, starts=None):
    pieces = []
    for base, start in zip(BASES, starts or (None, None)):
        piece = grid.fetch(shard if start is None else after(shard, start), base)
        pieces += [piece, grid.swap(piece, "dp", 1)]
    return pieces


def finish(grid, total):
    step = 2
    while step < grid.dps:
        total = total + grid.swap(total, "dp", step)
        step *= 2
    return total, grid.swap(total, "dp", 1)


def sum_two(grid, mine, away, others=()):
    mine = after(mine + grid.swap(away, "col", 1), *others)
    total, step = mine, 2
    while step < grid.cols:
        total = total + grid.swap(total, "col", step)
        step *= 2
    return mine, total


def sum_axis(grid, array, axis, step):
    while step < lax.axis_size(axis):
        array = array + grid.swap(array, axis, step)
        step *= 2
    return array


def dot(left, right, contract):
    return lax.dot_general(left, right, ((contract[:1], contract[1:]), ((), ())), preferred_element_type=F32)


def normalize(values):
    mean_part = jnp.mean(values, axis=-1, keepdims=True)
    square_part = jnp.mean(values * values, axis=-1, keepdims=True)
    inverse = lax.rsqrt(square_part - mean_part * mean_part + EPS)
    return (values - mean_part) * inverse, inverse


def norm_back(grad_normed, centred, inverse, norm_gain):
    scaled = grad_normed * norm_gain
    first_mean = jnp.mean(scaled, axis=-1, keepdims=True)
    second_mean = jnp.mean(scaled * centred, axis=-1, keepdims=True)
    return inverse * (scaled - first_mean - centred * second_mean)


def gelu_parts(pre_act):
    cdf_value = 0.5 * (1.0 + lax.erf(pre_act * 0.7071067811865476))
    density = jnp.exp(-0.5 * pre_act * pre_act) * 0.3989422804014327
    return (pre_act * cdf_value, cdf_value + pre_act * density)


def columns_sum(values):
    return jnp.sum(values, axis=0, keepdims=True)


def low_lanes(shape):
    return lax.broadcasted_iota(jnp.int32, shape, len(shape) - 1) % LANES < HD


def low(values):
    return jnp.where(low_lanes(values.shape), values, jnp.zeros_like(values))


def high(values):
    return jnp.where(low_lanes(values.shape), jnp.zeros_like(values), values)


def piece_rows(ids, which, size):
    side = ids[1] if which % 2 == 0 else 1 - ids[1]
    return pl.ds(pl.multiple_of((ids[0] ^ (BASES[which // 2] + side)) * size, size), size)


def copies(ids, pieces, full, sems, column=0):
    columns = pl.ds(column, full.shape[1])
    return [
        pltpu.make_async_copy(piece.at[:, columns], full.at[piece_rows(ids, i, piece.shape[0])], sems.at[i])
        for i, piece in enumerate(pieces)
    ]


def place(ids, pieces, full, sems, column=0):
    for copy in copies(ids, pieces, full, sems, column):
        copy.start()
    for copy in copies(ids, pieces, full, sems, column):
        copy.wait()


def place_proj(full, proj):
    one, two, three = (full[:, i * LANES : (i + 1) * LANES].astype(F32) for i in (1, 3, 5))
    proj[:, :LANES] = jnp.where(low_lanes(one.shape), pltpu.roll(one, HD, 1), two).astype(BF)
    proj[:, LANES:] = low(pltpu.roll(three, HD, 1)).astype(BF)


def split_halves(ids, values, mine, away):
    half = values.shape[1] // 2
    left, right = values[:, :half], values[:, half:]
    first = ids[0] % 2 == 0
    mine[...] = jnp.where(first, left, right)
    away[...] = jnp.where(first, right, left)


def join_halves(ids, mine, other):
    first = ids[0] % 2 == 0
    a, b = mine[...].astype(F32), other[...].astype(F32)
    return jnp.concatenate([jnp.where(first, a, b), jnp.where(first, b, a)], axis=1)


def close_kernel(ids, one, two, query, key, value, proj, query_bias, value_bias, proj_bias, gain, shift, hidden_bias, last_bias):
    total = one[...].astype(F32) + two[...].astype(F32)
    size, wide = query.shape
    step = wide + HD
    for i, ref in enumerate((query, key, value)):
        ref[...] = total[:size, i * step : i * step + wide]
    proj[...] = jnp.concatenate([total[:size, i * step + wide : (i + 1) * step] for i in range(3)], axis=1).T
    sums = total[size:]
    gain[...], shift[...], hidden_bias[...] = sums[0], sums[1], sums[4]
    query_bias[...], value_bias[...] = sums[3, :wide], sums[3, 2 * step : 2 * step + wide]
    for ref, row in ((proj_bias, sums[2:3]), (last_bias, sums[5:6])):
        mine = row[:, :wide]
        for i in range(1, row.shape[1] // wide):
            mine = jnp.where(ids[0] == i, row[:, i * wide : (i + 1) * wide], mine)
        ref[...] = mine[0]


def enter_kernel(tokens, cot, gain, shift, tokens_out, first_out, cot_out, sums):
    images = tokens.shape[0] // SEQ
    total = jnp.zeros((1, tokens.shape[1]), F32)
    for i in range(images):
        blank = jnp.zeros((PAD - SEQ, tokens.shape[1]), F32)
        here = pl.ds(i * PAD, PAD)
        rows = jnp.concatenate([tokens[pl.ds(i * SEQ, SEQ), :].astype(F32), blank], axis=0)
        tokens_out[here, :] = rows.astype(BF)
        centred, _ = normalize(rows)
        first_out[here, :] = (centred * gain[...] + shift[...]).astype(BF)
        rows = jnp.concatenate([cot[pl.ds(i * SEQ, SEQ), :].astype(F32), blank], axis=0)
        cot_out[here, :] = rows.astype(BF)
        total += columns_sum(rows)
    sums[...] = total


def attend_kernel(ids, first, h0, h1, h2, h3, bias, proj_bias, joined, attended, probs, mine, away, full, proj, sems):
    @pl.when(pl.program_id(0) == 0)
    def _():
        place(ids, (h0, h1, h2, h3), full, sems)
        place_proj(full, proj)

    rows = (dot(first[...], full[...], (1, 0)) + bias[...]).astype(BF)
    query = rows[:, : 2 * LANES] * jnp.asarray(HD**-0.5, BF)
    joined[:, : 2 * LANES] = query
    joined[:, 2 * LANES :] = rows[:, 2 * LANES :]
    key, value = rows[:, 2 * LANES : 4 * LANES], rows[:, 4 * LANES :]
    is_key = lax.broadcasted_iota(jnp.int32, (PAD, PAD), 1) < SEQ
    outs = []
    for head in range(3):
        lanes = slice(head // 2 * LANES, (head // 2 + 1) * LANES)
        part = high if head == 1 else low
        scores = dot(query[:, lanes], part(key[:, lanes]), (1, 1))
        scores = jnp.where(is_key, scores, -1e30)
        weights = jnp.exp(scores - jnp.max(scores, axis=-1, keepdims=True))
        weights = (weights * (1.0 / jnp.sum(weights, axis=-1, keepdims=True))).astype(BF)
        probs[head] = weights
        outs.append(dot(weights, part(value[:, lanes]), (1, 0)))
    result = jnp.concatenate([outs[0] + outs[1], outs[2]], axis=1).astype(BF)
    attended[...] = result
    split_halves(ids, (dot(result, proj[...], (1, 1)) + proj_bias[...]).astype(BF), mine, away)


def mlp_kernel(
    ids, tokens, one, two, cot, gain, shift, bias, w0, w1, w2, w3,
    second_out, hidden_out, pre_out, mine, away, sums, full, sems
):
    @pl.when(pl.program_id(0) == 0)
    def _():
        for copy in copies(ids, (w0, w1, w2, w3), full, sems):
            copy.start()
        sums[...] = jnp.zeros_like(sums)

    mid = tokens[...].astype(F32) + join_halves(ids, one, two)
    centred, _ = normalize(mid)
    second = (centred * gain[...] + shift[...]).astype(BF)
    second_out[...] = second

    @pl.when(pl.program_id(0) == 0)
    def _():
        for copy in copies(ids, (w0, w1, w2, w3), full, sems):
            copy.wait()

    width = hidden_out.shape[1]
    activ, slope = gelu_parts(dot(second, full[:, :width], (1, 0)) + bias[...])
    hidden_out[...] = activ.astype(BF)
    grad_pre = dot(cot[...], full[:, width:], (1, 0)) * slope
    sums[...] += columns_sum(grad_pre)
    grad_pre = grad_pre.astype(BF)
    pre_out[...] = grad_pre
    split_halves(ids, dot(grad_pre, full[:, :width], (1, 1)).astype(BF), mine, away)


def shrink_kernel(ids, hidden, w0, w1, w2, w3, bias, mine, away, shrink, sems):
    @pl.when(pl.program_id(0) == 0)
    def _():
        place(ids, (w0, w1, w2, w3), shrink, sems, hidden.shape[1])

    split_halves(ids, (dot(hidden[...], shrink[...], (1, 1)) + bias[...]).astype(BF), mine, away)


def deal(ids, full, stay_one, stay_two, away_one, away_two):
    size = stay_one.shape[0]
    for i, ref in enumerate((stay_one, away_one, stay_two, away_two)):
        ref[...] = full[piece_rows(ids, i, size), :].astype(BF)


def outer_kernel(ids, cot, hidden, second, grad_pre, s0, s1, a0, a1, full):
    width = hidden.shape[1]
    full[:, :width] = dot(second[...], grad_pre[...], (0, 0)).astype(BF)
    full[:, width:] = dot(cot[...], hidden[...], (0, 0)).astype(BF)
    deal(ids, full, s0, s1, a0, a1)


def joined_outer_kernel(ids, first, joined, grad_mid, attended, sums, pre_sum, cot_sum, s0, s1, away, full):
    full[...] = dot(first[...], joined[...], (0, 0)).astype(BF)
    other = dot(grad_mid[...], attended[...], (0, 0))
    turned = (pltpu.roll(other[:, :LANES], HD, 1), other[:, :LANES], pltpu.roll(other[:, LANES:], HD, 1))
    for i, values in enumerate(turned):
        lanes = pl.ds((2 * i + 1) * LANES, LANES)
        is_low = low_lanes(values.shape)
        full[:, lanes] = jnp.where(is_low, full[:, lanes].astype(F32), values).astype(BF)
    size = s0.shape[0] - SUMS
    blank = jnp.zeros((SUMS - 6, full.shape[1]), F32)
    below = jnp.concatenate([sums[...], pre_sum[...], cot_sum[...], blank], axis=0).astype(BF)
    places = (s0, s1, away.at[pl.ds(0, size + SUMS)], away.at[pl.ds(size + SUMS, size + SUMS)])
    deal(ids, full, *(ref.at[pl.ds(0, size)] for ref in places))
    for ref in places:
        ref[pl.ds(size, SUMS), :] = below


def attend_back_kernel(
    ids, one, two, tokens, mid_one, mid_two, cot, gain, h0, h1, h2, h3, joined, probs,
    grad_mid_out, grad_joined_out, mine, away, sums, full, proj, sems
):
    @pl.when(pl.program_id(0) == 0)
    def _():
        for copy in copies(ids, (h0, h1, h2, h3), full, sems):
            copy.start()
        sums[...] = jnp.zeros_like(sums)

    grad_normed = join_halves(ids, one, two)
    centred, inverse = normalize(tokens[...].astype(F32) + join_halves(ids, mid_one, mid_two))
    grad_mid = cot[...].astype(F32) + norm_back(grad_normed, centred, inverse, gain[...])
    grad_mid_b = grad_mid.astype(BF)
    grad_mid_out[...] = grad_mid_b

    @pl.when(pl.program_id(0) == 0)
    def _():
        for copy in copies(ids, (h0, h1, h2, h3), full, sems):
            copy.wait()
        place_proj(full, proj)

    grad_att = dot(grad_mid_b, proj[...], (1, 0)).astype(BF)
    query, key, value = (joined[:, i * 2 * LANES : (i + 1) * 2 * LANES] for i in range(3))
    queries, keys, values = [], [], []
    for head in range(3):
        lanes = slice(head // 2 * LANES, (head // 2 + 1) * LANES)
        part = high if head == 1 else low
        weights = probs[head]
        wide = weights.astype(F32)
        grad_weights = dot(grad_att[:, lanes], part(value[:, lanes]), (1, 1))
        row_delta = jnp.sum(wide * grad_weights, axis=-1, keepdims=True)
        grad_scores = (wide * (grad_weights - row_delta)).astype(BF)
        queries.append(dot(grad_scores, part(key[:, lanes]), (1, 0)))
        keys.append(dot(grad_scores, part(query[:, lanes]), (0, 0)))
        values.append(dot(weights, part(grad_att[:, lanes]), (0, 0)))
    scale = HD**-0.5
    result = jnp.concatenate(
        [(queries[0] + queries[1]) * scale, queries[2] * scale, keys[0] + keys[1], keys[2], values[0] + values[1], values[2]],
        axis=1,
    )
    for i, terms in enumerate((grad_normed * centred, grad_normed, grad_mid, result)):
        sums[i : i + 1, :] += columns_sum(terms)
    result = result.astype(BF)
    grad_joined_out[...] = result
    split_halves(ids, dot(result, full[...], (1, 1)).astype(BF), mine, away)


def leave(values, out):
    images = values.shape[0] // PAD
    out[...] = jnp.concatenate([values[i * PAD : i * PAD + SEQ] for i in range(images)], axis=0).astype(out.dtype)


def output_kernel(ids, one, two, tokens, mid_one, mid_two, out):
    mid = tokens[...].astype(F32) + join_halves(ids, mid_one, mid_two)
    leave(mid + join_halves(ids, one, two), out)


def exit_kernel(ids, one, upper, lower, grad_mid, tokens, gain, out, sums):
    two = jnp.concatenate([upper[...].astype(F32), lower[...].astype(F32)], axis=0)
    grad_normed = join_halves(ids, one, two)
    centred, inverse = normalize(tokens[...].astype(F32))
    leave(grad_mid[...].astype(F32) + norm_back(grad_normed, centred, inverse, gain[...]), out)
    sums[...] = jnp.concatenate([columns_sum(grad_normed * centred), columns_sum(grad_normed)], axis=0)


def run(kernel, ids, args, outs, flops, images=None, scratch=()):
    def spec(shape, how):
        if how == 3:
            return pl.BlockSpec(memory_space=pltpu.SMEM)
        if how == 2:
            return pl.BlockSpec(memory_space=pl.ANY)
        if images is None:
            return pl.BlockSpec(memory_space=pltpu.VMEM)
        if how == 0:
            return pl.BlockSpec(shape, lambda i: (0,) * len(shape))
        return pl.BlockSpec((shape[0] // images, *shape[1:]), lambda i: (i,) + (0,) * (len(shape) - 1))

    in_specs = [spec(a.shape, how) for a, how in args]
    arrays = [a for a, _ in args]
    if ids is not None:
        in_specs = [pl.BlockSpec(memory_space=pltpu.SMEM)] + in_specs
        arrays = [ids] + arrays
    size = sum(a.size * a.dtype.itemsize for a in arrays)
    shapes = [jax.ShapeDtypeStruct(*s) for s, _ in outs]
    size += sum(s.size * s.dtype.itemsize for s in shapes)
    how = {} if images is None else {"grid": (images,)}
    return list(pl.pallas_call(
        kernel,
        out_shape=shapes,
        in_specs=in_specs,
        out_specs=[spec(s[0], how) for s, how in outs],
        scratch_shapes=list(scratch),
        compiler_params=pltpu.CompilerParams(vmem_limit_bytes=52 * 1024 * 1024),
        cost_estimate=pl.CostEstimate(flops=1, bytes_accessed=1, transcendentals=0),
        **how,
    )(*arrays))


def on_device(
    tokens,
    attn_gain,
    attn_shift,
    query_weight,
    key_weight,
    value_weight,
    query_bias,
    value_bias,
    proj_weight,
    proj_bias,
    mlp_gain,
    mlp_shift,
    expand_weight,
    expand_bias,
    shrink_weight,
    shrink_bias,
    cotangent,
):
    grid = Grid()
    ids = grid.ids
    wide = query_weight.shape[1]
    model = tokens.shape[1]
    hidden_here = expand_weight.shape[1]
    images = tokens.shape[0] // SEQ
    rows = images * PAD
    heads = wide // HD
    half = model // 2
    assert heads == 3

    def pack(query, key, value, proj):
        parts = []
        for i, array in enumerate((query, key, value)):
            parts += [array, proj[..., i * HD : (i + 1) * HD]]
        return jnp.concatenate(parts, axis=-1)

    packed = pack(query_weight, key_weight, value_weight, proj_weight.T)
    both = jnp.concatenate([expand_weight, shrink_weight], axis=1)
    biases = grid.fetch_own(jnp.concatenate([query_bias, value_bias, expand_bias]))
    p_pieces = gather_block(grid, packed)
    w_pieces = gather_block(grid, after(both, p_pieces[0], p_pieces[2]))
    p_pieces[0] = after(p_pieces[0], w_pieces[0])
    q_bias, v_bias, e_bias = biases[:wide], biases[wide : 2 * wide], biases[2 * wide :]
    nothing = jnp.zeros_like(q_bias)
    joined_bias = pack(q_bias, nothing, v_bias, nothing)

    def line(vector):
        return vector.reshape(1, -1)

    def spread(bias):
        own = jnp.arange(model) // bias.shape[0] == grid.col
        return line(jnp.where(own, jnp.tile(bias, grid.cols), 0.0))

    tokens_pad, first_in, cot, cot_sum = run(
        enter_kernel,
        None,
        [(tokens, 0), (cotangent, 0), (line(attn_gain), 0), (line(attn_shift), 0)],
        [(((rows, model), BF), 0), (((rows, model), BF), 0), (((rows, model), BF), 0), (((1, model), F32), 0)],
        rows * model * 20,
    )
    weights_scratch = [pltpu.VMEM((model, model), BF), pltpu.VMEM((model, 2 * LANES), BF)]
    halves = [(((rows, half), BF), 1), (((rows, half), BF), 1)]
    joined, attended, probs, mine, away = run(
        attend_kernel,
        ids,
        [(first_in, 1)] + [(a, 2) for a in p_pieces] + [(line(joined_bias), 0), (spread(proj_bias), 0)],
        [
            (((rows, model), BF), 1),
            (((rows, 2 * LANES), BF), 1),
            (((heads * images, PAD, PAD), BF), 1),
        ]
        + halves,
        2 * rows * model * (model + 2 * wide),
        images,
        weights_scratch + [pltpu.SemaphoreType.DMA((4,))],
    )
    _, one = sum_two(grid, mine, away, (w_pieces[1], w_pieces[2]))
    two = grid.swap(after(one, w_pieces[3]), "col", 1)
    mid_one, mid_two = one, two
    second_in, hidden, grad_pre, mine, away, mlp_sums = run(
        mlp_kernel,
        ids,
        [(tokens_pad, 1), (one, 1), (two, 1), (cot, 1)]
        + [(line(a), 0) for a in (mlp_gain, mlp_shift, e_bias)]
        + [(a, 2) for a in w_pieces],
        [
            (((rows, model), BF), 1),
            (((rows, hidden_here), BF), 1),
            (((rows, hidden_here), BF), 1),
        ]
        + halves
        + [(((1, hidden_here), F32), 0)],
        2 * rows * model * hidden_here * 3,
        images,
        [pltpu.VMEM((model, 2 * hidden_here), BF), pltpu.SemaphoreType.DMA((4,))],
    )

    def pieces(width, more=0):
        return [(((model // grid.cols + more, width), BF), 0)] * 4

    mine, one = sum_two(grid, mine, away)
    hidden = after(hidden, mine)
    parts = run(
        outer_kernel,
        ids,
        [(cot, 0), (hidden, 0), (second_in, 0), (grad_pre, 0)],
        pieces(2 * hidden_here),
        4 * rows * model * hidden_here,
        scratch=[pltpu.VMEM((model, 2 * hidden_here), BF)],
    )
    got = [grid.swap(a, "dp", 1) for a in parts[2:]]
    mine_out, away_out = run(
        shrink_kernel,
        ids,
        [(after(hidden, parts[0]), 1)] + [(a, 2) for a in w_pieces] + [(spread(shrink_bias), 0)],
        halves,
        2 * rows * model * hidden_here,
        images,
        [pltpu.VMEM((model, hidden_here), BF), pltpu.SemaphoreType.DMA((4,))],
    )
    _, out_one = sum_two(grid, mine_out, away_out)
    one = after(one, away_out)
    two = grid.swap(one, "col", 1)

    taller = model // grid.cols + SUMS
    grad_mid, grad_joined, mine, away, back_sums = run(
        attend_back_kernel,
        ids,
        [(a, 1) for a in (one, two, tokens_pad, mid_one, mid_two, cot)]
        + [(line(mlp_gain), 0)]
        + [(a, 2) for a in p_pieces]
        + [(joined, 1), (probs, 1)],
        [(((rows, model), BF), 1)] * 2 + halves + [(((4, model), F32), 0)],
        2 * rows * model * (model + 2 * wide),
        images,
        weights_scratch + [pltpu.SemaphoreType.DMA((4,))],
    )
    sooner = after(parts[0], grad_joined) + got[0]
    packed_parts = run(
        joined_outer_kernel,
        ids,
        [(first_in, 0), (grad_joined, 0), (grad_mid, 0), (attended, 0)]
        + [(back_sums, 0), (mlp_sums, 0), (cot_sum, 0)],
        pieces(model, SUMS)[:2] + [(((2 * (model // grid.cols + SUMS), model), BF), 0)],
        2 * rows * model * model,
        scratch=[pltpu.VMEM((model, model), BF)],
    )
    packed_got = grid.swap(packed_parts[2], "dp", 1)
    packed_got = packed_got[: model // grid.cols + SUMS], packed_got[model // grid.cols + SUMS :]
    later = after(parts[1], packed_parts[0]) + got[1]
    away = after(away, packed_parts[0], later, out_one)
    sooner, later = grid.give(sooner, BASES[0]), grid.give(later, BASES[1])
    mine, one = sum_two(grid, mine, away)
    (output,) = run(
        output_kernel,
        ids,
        [(after(out_one, mine), 0), (grid.swap(out_one, "col", 1), 0)]
        + [(a, 0) for a in (tokens_pad, mid_one, mid_two)],
        [((tokens.shape, BF), 0)],
        rows * model,
    )
    packed_one = after(packed_parts[0], output, sooner) + packed_got[0]
    packed_two = after(packed_parts[1], packed_one) + packed_got[1]
    packed_given = [grid.give(packed_one, BASES[0]), grid.give(packed_two, BASES[1])]
    total = after(sooner, packed_two, one) + later
    one = after(one, total)
    grad_tokens, late = run(
        exit_kernel,
        ids,
        [(after(one, packed_two), 0)]
        + [(grid.swap(part, "col", 1), 0) for part in (one[:CUT], one[CUT:])]
        + [(grad_mid, 0), (tokens_pad, 0), (line(attn_gain), 0)],
        [((tokens.shape, BF), 0), (((2, model), F32), 0)],
        rows * model * 20,
    )
    own, other = finish(grid, total)
    grad_both = own.astype(F32) + other.astype(F32)
    packed_total = after(packed_given[0], grad_tokens) + packed_given[1]
    own, other = finish(grid, packed_total)
    late = sum_axis(grid, after(late, packed_total), "row", 1)
    late = sum_axis(grid, after(late, grad_both), "dp", 1)
    square, line_of = (query_weight.shape, F32), lambda size: (((size,), F32), 0)
    (
        grad_query,
        grad_key,
        grad_value,
        grad_proj,
        grad_query_bias,
        grad_value_bias,
        grad_proj_bias,
        grad_mlp_gain,
        grad_mlp_shift,
        grad_expand_bias,
        grad_shrink_bias,
    ) = run(
        close_kernel,
        ids,
        [(own, 0), (other, 0)],
        [(square, 0)] * 4 + [line_of(wide)] * 3 + [line_of(model)] * 3 + [line_of(wide)],
        1,
    )
    return (
        output,
        grad_tokens,
        late[0],
        late[1],
        grad_query,
        grad_key,
        grad_value,
        grad_query_bias,
        grad_value_bias,
        grad_proj,
        grad_proj_bias,
        grad_mlp_gain,
        grad_mlp_shift,
        grad_both[:, :hidden_here],
        grad_expand_bias,
        grad_both[:, hidden_here:],
        grad_shrink_bias,
    )


def solution(mesh):
    placed = (
        P(("dp", "row"), None),
        P(),
        P(),
        P("col", "row"),
        P("col", "row"),
        P("col", "row"),
        P("row"),
        P("row"),
        P("row", "col"),
        P("col"),
        P(),
        P(),
        P("col", "row"),
        P("row"),
        P("col", "row"),
        P("col"),
        P(("dp", "row"), None),
    )
    return jax.shard_map(
        on_device,
        mesh=mesh,
        in_specs=placed,
        out_specs=(
            P(("dp", "row"), None),
            P(("dp", "row"), None),
            P(),
            P(),
            P("col", "row"),
            P("col", "row"),
            P("col", "row"),
            P("row"),
            P("row"),
            P("row", "col"),
            P("col"),
            P(),
            P(),
            P("col", "row"),
            P("row"),
            P("col", "row"),
            P("col"),
        ),
        check_vma=False,
    )
```

```python
import jax
import jax.numpy as jnp
from jax import lax
from jax.experimental import pallas as pl
from jax.experimental.pallas import tpu as pltpu
from jax.sharding import PartitionSpec as P

HD = 64
SEQ = 197
PAD = 208
LANES = 128
SUMS = 16
CUT = 320
EPS = 1e-06
BF = jnp.bfloat16
F32 = jnp.float32


def mirrored(index, size):
    out, step = 0, 1
    while step < size:
        out = out * 2 + (index // step) % 2
        step *= 2
    return out


class Grid:
    def __init__(self):
        self.rows = lax.axis_size("row")
        self.cols = lax.axis_size("col")
        self.dps = lax.axis_size("dp")
        assert self.rows == self.cols
        self.row = lax.axis_index("row")
        self.col = lax.axis_index("col")
        self.dp = lax.axis_index("dp")
        self.mirror = [mirrored(c, self.cols) for c in range(self.cols)]
        self.block = self.row ^ jnp.array(self.mirror, jnp.int32)[self.col]
        self.ids = jnp.stack([self.col, self.dp % 2]).astype(jnp.int32)

    def moves(self, base):
        for d in range(self.dps):
            for r in range(self.rows):
                for c in range(self.cols):
                    holder = (d * self.rows + (r ^ self.mirror[c])) * self.cols + (c ^ (base + d % 2))
                    yield (d * self.rows + r) * self.cols + c, holder

    def fetch(self, array, base):
        return lax.ppermute(array, ("dp", "row", "col"), [(holder, me) for me, holder in self.moves(base)])

    def give(self, array, base):
        return lax.ppermute(array, ("dp", "row", "col"), [(me, holder) for me, holder in self.moves(base)])

    def fetch_own(self, array):
        pairs = []
        for r in range(self.rows):
            for c in range(self.cols):
                pairs.append(((r ^ self.mirror[c]) * self.cols + c, r * self.cols + c))
        return lax.ppermute(array, ("row", "col"), pairs)

    def swap(self, array, axis, flip):
        size = lax.axis_size(axis)
        return lax.ppermute(array, axis, [(i, i ^ flip) for i in range(size)])


def after(value, *others):
    return lax.optimization_barrier((value, others))[0]


BASES = (2, 0)


def gather_block(grid, shard, starts=None):
    pieces = []
    for base, start in zip(BASES, starts or (None, None)):
        piece = grid.fetch(shard if start is None else after(shard, start), base)
        pieces += [piece, grid.swap(piece, "dp", 1)]
    return pieces


def finish(grid, total):
    step = 2
    while step < grid.dps:
        total = total + grid.swap(total, "dp", step)
        step *= 2
    return total, grid.swap(total, "dp", 1)


def sum_two(grid, mine, away, others=()):
    mine = after(mine + grid.swap(away, "col", 1), *others)
    total, step = mine, 2
    while step < grid.cols:
        total = total + grid.swap(total, "col", step)
        step *= 2
    return mine, total


def sum_axis(grid, array, axis, step):
    while step < lax.axis_size(axis):
        array = array + grid.swap(array, axis, step)
        step *= 2
    return array


def dot(left, right, contract):
    return lax.dot_general(left, right, ((contract[:1], contract[1:]), ((), ())), preferred_element_type=F32)


def normalize(values):
    mean_part = jnp.mean(values, axis=-1, keepdims=True)
    square_part = jnp.mean(values * values, axis=-1, keepdims=True)
    inverse = lax.rsqrt(square_part - mean_part * mean_part + EPS)
    return (values - mean_part) * inverse, inverse


def norm_back(grad_normed, centred, inverse, norm_gain):
    scaled = grad_normed * norm_gain
    first_mean = jnp.mean(scaled, axis=-1, keepdims=True)
    second_mean = jnp.mean(scaled * centred, axis=-1, keepdims=True)
    return inverse * (scaled - first_mean - centred * second_mean)


def gelu_parts(pre_act):
    cdf_value = 0.5 * (1.0 + lax.erf(pre_act * 0.7071067811865476))
    density = jnp.exp(-0.5 * pre_act * pre_act) * 0.3989422804014327
    return (pre_act * cdf_value, cdf_value + pre_act * density)


def columns_sum(values):
    return jnp.sum(values, axis=0, keepdims=True)


def low_lanes(shape):
    return lax.broadcasted_iota(jnp.int32, shape, len(shape) - 1) % LANES < HD


def low(values):
    return jnp.where(low_lanes(values.shape), values, jnp.zeros_like(values))


def high(values):
    return jnp.where(low_lanes(values.shape), jnp.zeros_like(values), values)


def piece_rows(ids, which, size):
    side = ids[1] if which % 2 == 0 else 1 - ids[1]
    return pl.ds(pl.multiple_of((ids[0] ^ (BASES[which // 2] + side)) * size, size), size)


def copies(ids, pieces, full, sems, column=0):
    columns = pl.ds(column, full.shape[1])
    return [
        pltpu.make_async_copy(piece.at[:, columns], full.at[piece_rows(ids, i, piece.shape[0])], sems.at[i])
        for i, piece in enumerate(pieces)
    ]


def place(ids, pieces, full, sems, column=0):
    for copy in copies(ids, pieces, full, sems, column):
        copy.start()
    for copy in copies(ids, pieces, full, sems, column):
        copy.wait()


def place_proj(full, proj):
    one, two, three = (full[:, i * LANES : (i + 1) * LANES].astype(F32) for i in (1, 3, 5))
    proj[:, :LANES] = jnp.where(low_lanes(one.shape), pltpu.roll(one, HD, 1), two).astype(BF)
    proj[:, LANES:] = low(pltpu.roll(three, HD, 1)).astype(BF)


def split_halves(ids, values, mine, away):
    half = values.shape[1] // 2
    left, right = values[:, :half], values[:, half:]
    first = ids[0] % 2 == 0
    mine[...] = jnp.where(first, left, right)
    away[...] = jnp.where(first, right, left)


def join_halves(ids, mine, other):
    first = ids[0] % 2 == 0
    a, b = mine[...].astype(F32), other[...].astype(F32)
    return jnp.concatenate([jnp.where(first, a, b), jnp.where(first, b, a)], axis=1)


def close_kernel(ids, one, two, query, key, value, proj, query_bias, value_bias, proj_bias, gain, shift, hidden_bias, last_bias):
    total = one[...].astype(F32) + two[...].astype(F32)
    size, wide = query.shape
    step = wide + HD
    for i, ref in enumerate((query, key, value)):
        ref[...] = total[:size, i * step : i * step + wide]
    proj[...] = jnp.concatenate([total[:size, i * step + wide : (i + 1) * step] for i in range(3)], axis=1).T
    sums = total[size:]
    gain[...], shift[...], hidden_bias[...] = sums[0], sums[1], sums[4]
    query_bias[...], value_bias[...] = sums[3, :wide], sums[3, 2 * step : 2 * step + wide]
    for ref, row in ((proj_bias, sums[2:3]), (last_bias, sums[5:6])):
        mine = row[:, :wide]
        for i in range(1, row.shape[1] // wide):
            mine = jnp.where(ids[0] == i, row[:, i * wide : (i + 1) * wide], mine)
        ref[...] = mine[0]


def enter_kernel(tokens, cot, gain, shift, tokens_out, first_out, cot_out, sums):
    images = tokens.shape[0] // SEQ
    total = jnp.zeros((1, tokens.shape[1]), F32)
    for i in range(images):
        blank = jnp.zeros((PAD - SEQ, tokens.shape[1]), F32)
        here = pl.ds(i * PAD, PAD)
        rows = jnp.concatenate([tokens[pl.ds(i * SEQ, SEQ), :].astype(F32), blank], axis=0)
        tokens_out[here, :] = rows.astype(BF)
        centred, _ = normalize(rows)
        first_out[here, :] = (centred * gain[...] + shift[...]).astype(BF)
        rows = jnp.concatenate([cot[pl.ds(i * SEQ, SEQ), :].astype(F32), blank], axis=0)
        cot_out[here, :] = rows.astype(BF)
        total += columns_sum(rows)
    sums[...] = total


def attend_kernel(ids, first, h0, h1, h2, h3, bias, proj_bias, joined, attended, probs, mine, away, full, proj, sems):
    @pl.when(pl.program_id(0) == 0)
    def _():
        place(ids, (h0, h1, h2, h3), full, sems)
        place_proj(full, proj)

    rows = (dot(first[...], full[...], (1, 0)) + bias[...]).astype(BF)
    query = rows[:, : 2 * LANES] * jnp.asarray(HD**-0.5, BF)
    joined[:, : 2 * LANES] = query
    joined[:, 2 * LANES :] = rows[:, 2 * LANES :]
    key, value = rows[:, 2 * LANES : 4 * LANES], rows[:, 4 * LANES :]
    is_key = lax.broadcasted_iota(jnp.int32, (PAD, PAD), 1) < SEQ
    outs = []
    for head in range(3):
        lanes = slice(head // 2 * LANES, (head // 2 + 1) * LANES)
        part = high if head == 1 else low
        scores = dot(query[:, lanes], part(key[:, lanes]), (1, 1))
        scores = jnp.where(is_key, scores, -1e30)
        weights = jnp.exp(scores - jnp.max(scores, axis=-1, keepdims=True))
        weights = (weights * (1.0 / jnp.sum(weights, axis=-1, keepdims=True))).astype(BF)
        probs[head] = weights
        outs.append(dot(weights, part(value[:, lanes]), (1, 0)))
    result = jnp.concatenate([outs[0] + outs[1], outs[2]], axis=1).astype(BF)
    attended[...] = result
    split_halves(ids, (dot(result, proj[...], (1, 1)) + proj_bias[...]).astype(BF), mine, away)


def mlp_kernel(
    ids, tokens, one, two, cot, gain, shift, bias, w0, w1, w2, w3,
    second_out, hidden_out, pre_out, mine, away, sums, full, sems
):
    @pl.when(pl.program_id(0) == 0)
    def _():
        for copy in copies(ids, (w0, w1, w2, w3), full, sems):
            copy.start()
        sums[...] = jnp.zeros_like(sums)

    mid = tokens[...].astype(F32) + join_halves(ids, one, two)
    centred, _ = normalize(mid)
    second = (centred * gain[...] + shift[...]).astype(BF)
    second_out[...] = second

    @pl.when(pl.program_id(0) == 0)
    def _():
        for copy in copies(ids, (w0, w1, w2, w3), full, sems):
            copy.wait()

    width = hidden_out.shape[1]
    activ, slope = gelu_parts(dot(second, full[:, :width], (1, 0)) + bias[...])
    hidden_out[...] = activ.astype(BF)
    grad_pre = dot(cot[...], full[:, width:], (1, 0)) * slope
    sums[...] += columns_sum(grad_pre)
    grad_pre = grad_pre.astype(BF)
    pre_out[...] = grad_pre
    split_halves(ids, dot(grad_pre, full[:, :width], (1, 1)).astype(BF), mine, away)


def shrink_kernel(ids, hidden, w0, w1, w2, w3, bias, mine, away, shrink, sems):
    @pl.when(pl.program_id(0) == 0)
    def _():
        place(ids, (w0, w1, w2, w3), shrink, sems, hidden.shape[1])

    split_halves(ids, (dot(hidden[...], shrink[...], (1, 1)) + bias[...]).astype(BF), mine, away)


def deal(ids, full, stay_one, stay_two, away_one, away_two):
    size = stay_one.shape[0]
    for i, ref in enumerate((stay_one, away_one, stay_two, away_two)):
        ref[...] = full[piece_rows(ids, i, size), :].astype(BF)


def outer_kernel(ids, cot, hidden, second, grad_pre, s0, s1, a0, a1, full):
    width = hidden.shape[1]
    full[:, :width] = dot(second[...], grad_pre[...], (0, 0)).astype(BF)
    full[:, width:] = dot(cot[...], hidden[...], (0, 0)).astype(BF)
    deal(ids, full, s0, s1, a0, a1)


def joined_outer_kernel(ids, first, joined, grad_mid, attended, sums, pre_sum, cot_sum, s0, s1, away, full):
    full[...] = dot(first[...], joined[...], (0, 0)).astype(BF)
    other = dot(grad_mid[...], attended[...], (0, 0))
    turned = (pltpu.roll(other[:, :LANES], HD, 1), other[:, :LANES], pltpu.roll(other[:, LANES:], HD, 1))
    for i, values in enumerate(turned):
        lanes = pl.ds((2 * i + 1) * LANES, LANES)
        is_low = low_lanes(values.shape)
        full[:, lanes] = jnp.where(is_low, full[:, lanes].astype(F32), values).astype(BF)
    size = s0.shape[0] - SUMS
    blank = jnp.zeros((SUMS - 6, full.shape[1]), F32)
    below = jnp.concatenate([sums[...], pre_sum[...], cot_sum[...], blank], axis=0).astype(BF)
    places = (s0, s1, away.at[pl.ds(0, size + SUMS)], away.at[pl.ds(size + SUMS, size + SUMS)])
    deal(ids, full, *(ref.at[pl.ds(0, size)] for ref in places))
    for ref in places:
        ref[pl.ds(size, SUMS), :] = below


def attend_back_kernel(
    ids, one, two, tokens, mid_one, mid_two, cot, gain, h0, h1, h2, h3, joined, probs,
    grad_mid_out, grad_joined_out, mine, away, sums, full, proj, sems
):
    @pl.when(pl.program_id(0) == 0)
    def _():
        for copy in copies(ids, (h0, h1, h2, h3), full, sems):
            copy.start()
        sums[...] = jnp.zeros_like(sums)

    grad_normed = join_halves(ids, one, two)
    centred, inverse = normalize(tokens[...].astype(F32) + join_halves(ids, mid_one, mid_two))
    grad_mid = cot[...].astype(F32) + norm_back(grad_normed, centred, inverse, gain[...])
    grad_mid_b = grad_mid.astype(BF)
    grad_mid_out[...] = grad_mid_b

    @pl.when(pl.program_id(0) == 0)
    def _():
        for copy in copies(ids, (h0, h1, h2, h3), full, sems):
            copy.wait()
        place_proj(full, proj)

    grad_att = dot(grad_mid_b, proj[...], (1, 0)).astype(BF)
    query, key, value = (joined[:, i * 2 * LANES : (i + 1) * 2 * LANES] for i in range(3))
    queries, keys, values = [], [], []
    for head in range(3):
        lanes = slice(head // 2 * LANES, (head // 2 + 1) * LANES)
        part = high if head == 1 else low
        weights = probs[head]
        wide = weights.astype(F32)
        grad_weights = dot(grad_att[:, lanes], part(value[:, lanes]), (1, 1))
        row_delta = jnp.sum(wide * grad_weights, axis=-1, keepdims=True)
        grad_scores = (wide * (grad_weights - row_delta)).astype(BF)
        queries.append(dot(grad_scores, part(key[:, lanes]), (1, 0)))
        keys.append(dot(grad_scores, part(query[:, lanes]), (0, 0)))
        values.append(dot(weights, part(grad_att[:, lanes]), (0, 0)))
    scale = HD**-0.5
    result = jnp.concatenate(
        [(queries[0] + queries[1]) * scale, queries[2] * scale, keys[0] + keys[1], keys[2], values[0] + values[1], values[2]],
        axis=1,
    )
    for i, terms in enumerate((grad_normed * centred, grad_normed, grad_mid, result)):
        sums[i : i + 1, :] += columns_sum(terms)
    result = result.astype(BF)
    grad_joined_out[...] = result
    split_halves(ids, dot(result, full[...], (1, 1)).astype(BF), mine, away)


def leave(values, out):
    images = values.shape[0] // PAD
    out[...] = jnp.concatenate([values[i * PAD : i * PAD + SEQ] for i in range(images)], axis=0).astype(out.dtype)


def output_kernel(ids, one, two, tokens, mid_one, mid_two, out):
    mid = tokens[...].astype(F32) + join_halves(ids, mid_one, mid_two)
    leave(mid + join_halves(ids, one, two), out)


def exit_kernel(ids, one, upper, lower, grad_mid, tokens, gain, out, sums):
    two = jnp.concatenate([upper[...].astype(F32), lower[...].astype(F32)], axis=0)
    grad_normed = join_halves(ids, one, two)
    centred, inverse = normalize(tokens[...].astype(F32))
    leave(grad_mid[...].astype(F32) + norm_back(grad_normed, centred, inverse, gain[...]), out)
    sums[...] = jnp.concatenate([columns_sum(grad_normed * centred), columns_sum(grad_normed)], axis=0)


def run(kernel, ids, args, outs, flops, images=None, scratch=()):
    def spec(shape, how):
        if how == 3:
            return pl.BlockSpec(memory_space=pltpu.SMEM)
        if how == 2:
            return pl.BlockSpec(memory_space=pl.ANY)
        if images is None:
            return pl.BlockSpec(memory_space=pltpu.VMEM)
        if how == 0:
            return pl.BlockSpec(shape, lambda i: (0,) * len(shape))
        return pl.BlockSpec((shape[0] // images, *shape[1:]), lambda i: (i,) + (0,) * (len(shape) - 1))

    in_specs = [spec(a.shape, how) for a, how in args]
    arrays = [a for a, _ in args]
    if ids is not None:
        in_specs = [pl.BlockSpec(memory_space=pltpu.SMEM)] + in_specs
        arrays = [ids] + arrays
    size = sum(a.size * a.dtype.itemsize for a in arrays)
    shapes = [jax.ShapeDtypeStruct(*s) for s, _ in outs]
    size += sum(s.size * s.dtype.itemsize for s in shapes)
    how = {} if images is None else {"grid": (images,)}
    return list(pl.pallas_call(
        kernel,
        out_shape=shapes,
        in_specs=in_specs,
        out_specs=[spec(s[0], how) for s, how in outs],
        scratch_shapes=list(scratch),
        compiler_params=pltpu.CompilerParams(vmem_limit_bytes=52 * 1024 * 1024),
        cost_estimate=pl.CostEstimate(flops=1, bytes_accessed=1, transcendentals=0),
        **how,
    )(*arrays))


def on_device(
    tokens,
    attn_gain,
    attn_shift,
    query_weight,
    key_weight,
    value_weight,
    query_bias,
    value_bias,
    proj_weight,
    proj_bias,
    mlp_gain,
    mlp_shift,
    expand_weight,
    expand_bias,
    shrink_weight,
    shrink_bias,
    cotangent,
):
    grid = Grid()
    ids = grid.ids
    wide = query_weight.shape[1]
    model = tokens.shape[1]
    hidden_here = expand_weight.shape[1]
    images = tokens.shape[0] // SEQ
    rows = images * PAD
    heads = wide // HD
    half = model // 2
    assert heads == 3

    def pack(query, key, value, proj):
        parts = []
        for i, array in enumerate((query, key, value)):
            parts += [array, proj[..., i * HD : (i + 1) * HD]]
        return jnp.concatenate(parts, axis=-1)

    packed = pack(query_weight, key_weight, value_weight, proj_weight.T)
    both = jnp.concatenate([expand_weight, shrink_weight], axis=1)
    biases = grid.fetch_own(jnp.concatenate([query_bias, value_bias, expand_bias]))
    p_pieces = gather_block(grid, packed)
    w_pieces = gather_block(grid, after(both, p_pieces[0], p_pieces[2]))
    p_pieces[0] = after(p_pieces[0], w_pieces[0])
    q_bias, v_bias, e_bias = biases[:wide], biases[wide : 2 * wide], biases[2 * wide :]
    nothing = jnp.zeros_like(q_bias)
    joined_bias = pack(q_bias, nothing, v_bias, nothing)

    def line(vector):
        return vector.reshape(1, -1)

    def spread(bias):
        own = jnp.arange(model) // bias.shape[0] == grid.col
        return line(jnp.where(own, jnp.tile(bias, grid.cols), 0.0))

    tokens_pad, first_in, cot, cot_sum = run(
        enter_kernel,
        None,
        [(tokens, 0), (cotangent, 0), (line(attn_gain), 0), (line(attn_shift), 0)],
        [(((rows, model), BF), 0), (((rows, model), BF), 0), (((rows, model), BF), 0), (((1, model), F32), 0)],
        rows * model * 20,
    )
    weights_scratch = [pltpu.VMEM((model, model), BF), pltpu.VMEM((model, 2 * LANES), BF)]
    halves = [(((rows, half), BF), 1), (((rows, half), BF), 1)]
    joined, attended, probs, mine, away = run(
        attend_kernel,
        ids,
        [(first_in, 1)] + [(a, 2) for a in p_pieces] + [(line(joined_bias), 0), (spread(proj_bias), 0)],
        [
            (((rows, model), BF), 1),
            (((rows, 2 * LANES), BF), 1),
            (((heads * images, PAD, PAD), BF), 1),
        ]
        + halves,
        2 * rows * model * (model + 2 * wide),
        images,
        weights_scratch + [pltpu.SemaphoreType.DMA((4,))],
    )
    _, one = sum_two(grid, mine, away, (w_pieces[1], w_pieces[2]))
    two = grid.swap(after(one, w_pieces[3]), "col", 1)
    mid_one, mid_two = one, two
    second_in, hidden, grad_pre, mine, away, mlp_sums = run(
        mlp_kernel,
        ids,
        [(tokens_pad, 1), (one, 1), (two, 1), (cot, 1)]
        + [(line(a), 0) for a in (mlp_gain, mlp_shift, e_bias)]
        + [(a, 2) for a in w_pieces],
        [
            (((rows, model), BF), 1),
            (((rows, hidden_here), BF), 1),
            (((rows, hidden_here), BF), 1),
        ]
        + halves
        + [(((1, hidden_here), F32), 0)],
        2 * rows * model * hidden_here * 3,
        images,
        [pltpu.VMEM((model, 2 * hidden_here), BF), pltpu.SemaphoreType.DMA((4,))],
    )

    def pieces(width, more=0):
        return [(((model // grid.cols + more, width), BF), 0)] * 4

    mine, one = sum_two(grid, mine, away)
    hidden = after(hidden, mine)
    parts = run(
        outer_kernel,
        ids,
        [(cot, 0), (hidden, 0), (second_in, 0), (grad_pre, 0)],
        pieces(2 * hidden_here),
        4 * rows * model * hidden_here,
        scratch=[pltpu.VMEM((model, 2 * hidden_here), BF)],
    )
    got = [grid.swap(a, "dp", 1) for a in parts[2:]]
    mine_out, away_out = run(
        shrink_kernel,
        ids,
        [(after(hidden, parts[0]), 1)] + [(a, 2) for a in w_pieces] + [(spread(shrink_bias), 0)],
        halves,
        2 * rows * model * hidden_here,
        images,
        [pltpu.VMEM((model, hidden_here), BF), pltpu.SemaphoreType.DMA((4,))],
    )
    _, out_one = sum_two(grid, mine_out, away_out)
    one = after(one, away_out)
    two = grid.swap(one, "col", 1)

    taller = model // grid.cols + SUMS
    grad_mid, grad_joined, mine, away, back_sums = run(
        attend_back_kernel,
        ids,
        [(a, 1) for a in (one, two, tokens_pad, mid_one, mid_two, cot)]
        + [(line(mlp_gain), 0)]
        + [(a, 2) for a in p_pieces]
        + [(joined, 1), (probs, 1)],
        [(((rows, model), BF), 1)] * 2 + halves + [(((4, model), F32), 0)],
        2 * rows * model * (model + 2 * wide),
        images,
        weights_scratch + [pltpu.SemaphoreType.DMA((4,))],
    )
    sooner = after(parts[0], grad_joined) + got[0]
    packed_parts = run(
        joined_outer_kernel,
        ids,
        [(first_in, 0), (grad_joined, 0), (grad_mid, 0), (attended, 0)]
        + [(back_sums, 0), (mlp_sums, 0), (cot_sum, 0)],
        pieces(model, SUMS)[:2] + [(((2 * (model // grid.cols + SUMS), model), BF), 0)],
        2 * rows * model * model,
        scratch=[pltpu.VMEM((model, model), BF)],
    )
    packed_got = grid.swap(packed_parts[2], "dp", 1)
    packed_got = packed_got[: model // grid.cols + SUMS], packed_got[model // grid.cols + SUMS :]
    later = after(parts[1], packed_parts[0]) + got[1]
    away = after(away, packed_parts[0], later, out_one)
    sooner, later = grid.give(sooner, BASES[0]), grid.give(later, BASES[1])
    mine, one = sum_two(grid, mine, away)
    (output,) = run(
        output_kernel,
        ids,
        [(after(out_one, mine), 0), (grid.swap(out_one, "col", 1), 0)]
        + [(a, 0) for a in (tokens_pad, mid_one, mid_two)],
        [((tokens.shape, BF), 0)],
        rows * model,
    )
    packed_one = after(packed_parts[0], output, sooner) + packed_got[0]
    packed_two = after(packed_parts[1], packed_one) + packed_got[1]
    packed_given = [grid.give(packed_one, BASES[0]), grid.give(packed_two, BASES[1])]
    total = after(sooner, packed_two, one) + later
    one = after(one, total)
    grad_tokens, late = run(
        exit_kernel,
        ids,
        [(after(one, packed_two), 0)]
        + [(grid.swap(part, "col", 1), 0) for part in (one[:CUT], one[CUT:])]
        + [(grad_mid, 0), (tokens_pad, 0), (line(attn_gain), 0)],
        [((tokens.shape, BF), 0), (((2, model), F32), 0)],
        rows * model * 20,
    )
    own, other = finish(grid, total)
    grad_both = own.astype(F32) + other.astype(F32)
    packed_total = after(packed_given[0], grad_tokens) + packed_given[1]
    own, other = finish(grid, packed_total)
    late = sum_axis(grid, after(late, packed_total), "row", 1)
    late = sum_axis(grid, late, "dp", 1)
    square, line_of = (query_weight.shape, F32), lambda size: (((size,), F32), 0)
    (
        grad_query,
        grad_key,
        grad_value,
        grad_proj,
        grad_query_bias,
        grad_value_bias,
        grad_proj_bias,
        grad_mlp_gain,
        grad_mlp_shift,
        grad_expand_bias,
        grad_shrink_bias,
    ) = run(
        close_kernel,
        ids,
        [(own, 0), (other, 0)],
        [(square, 0)] * 4 + [line_of(wide)] * 3 + [line_of(model)] * 3 + [line_of(wide)],
        1,
    )
    return (
        output,
        grad_tokens,
        late[0],
        late[1],
        grad_query,
        grad_key,
        grad_value,
        grad_query_bias,
        grad_value_bias,
        grad_proj,
        grad_proj_bias,
        grad_mlp_gain,
        grad_mlp_shift,
        grad_both[:, :hidden_here],
        grad_expand_bias,
        grad_both[:, hidden_here:],
        grad_shrink_bias,
    )


def solution(mesh):
    placed = (
        P(("dp", "row"), None),
        P(),
        P(),
        P("col", "row"),
        P("col", "row"),
        P("col", "row"),
        P("row"),
        P("row"),
        P("row", "col"),
        P("col"),
        P(),
        P(),
        P("col", "row"),
        P("row"),
        P("col", "row"),
        P("col"),
        P(("dp", "row"), None),
    )
    return jax.shard_map(
        on_device,
        mesh=mesh,
        in_specs=placed,
        out_specs=(
            P(("dp", "row"), None),
            P(("dp", "row"), None),
            P(),
            P(),
            P("col", "row"),
            P("col", "row"),
            P("col", "row"),
            P("row"),
            P("row"),
            P("row", "col"),
            P("col"),
            P(),
            P(),
            P("col", "row"),
            P("row"),
            P("col", "row"),
            P("col"),
        ),
        check_vma=False,
    )
```

```python
import jax
import jax.numpy as jnp
from jax import lax
from jax.experimental import pallas as pl
from jax.experimental.pallas import tpu as pltpu
from jax.sharding import PartitionSpec as P

HD = 64
SEQ = 197
PAD = 208
LANES = 128
SUMS = 16
CUT = 320
EPS = 1e-06
BF = jnp.bfloat16
F32 = jnp.float32


def mirrored(index, size):
    out, step = 0, 1
    while step < size:
        out = out * 2 + (index // step) % 2
        step *= 2
    return out


class Grid:
    def __init__(self):
        self.rows = lax.axis_size("row")
        self.cols = lax.axis_size("col")
        self.dps = lax.axis_size("dp")
        assert self.rows == self.cols
        self.row = lax.axis_index("row")
        self.col = lax.axis_index("col")
        self.dp = lax.axis_index("dp")
        self.mirror = [mirrored(c, self.cols) for c in range(self.cols)]
        self.block = self.row ^ jnp.array(self.mirror, jnp.int32)[self.col]
        self.ids = jnp.stack([self.col, self.dp % 2]).astype(jnp.int32)

    def moves(self, base):
        for d in range(self.dps):
            for r in range(self.rows):
                for c in range(self.cols):
                    holder = (d * self.rows + (r ^ self.mirror[c])) * self.cols + (c ^ (base + d % 2))
                    yield (d * self.rows + r) * self.cols + c, holder

    def fetch(self, array, base):
        return lax.ppermute(array, ("dp", "row", "col"), [(holder, me) for me, holder in self.moves(base)])

    def give(self, array, base):
        return lax.ppermute(array, ("dp", "row", "col"), [(me, holder) for me, holder in self.moves(base)])

    def fetch_own(self, array):
        pairs = []
        for r in range(self.rows):
            for c in range(self.cols):
                pairs.append(((r ^ self.mirror[c]) * self.cols + c, r * self.cols + c))
        return lax.ppermute(array, ("row", "col"), pairs)

    def swap(self, array, axis, flip):
        size = lax.axis_size(axis)
        return lax.ppermute(array, axis, [(i, i ^ flip) for i in range(size)])


def after(value, *others):
    return lax.optimization_barrier((value, others))[0]


BASES = (2, 0)


def gather_block(grid, shard, starts=None):
    pieces = []
    for base, start in zip(BASES, starts or (None, None)):
        piece = grid.fetch(shard if start is None else after(shard, start), base)
        pieces += [piece, grid.swap(piece, "dp", 1)]
    return pieces


def finish(grid, total):
    step = 2
    while step < grid.dps:
        total = total + grid.swap(total, "dp", step)
        step *= 2
    return total, grid.swap(total, "dp", 1)


def sum_two(grid, mine, away, others=()):
    mine = after(mine + grid.swap(away, "col", 1), *others)
    total, step = mine, 2
    while step < grid.cols:
        total = total + grid.swap(total, "col", step)
        step *= 2
    return mine, total


def sum_axis(grid, array, axis, step):
    while step < lax.axis_size(axis):
        array = array + grid.swap(array, axis, step)
        step *= 2
    return array


def dot(left, right, contract):
    return lax.dot_general(left, right, ((contract[:1], contract[1:]), ((), ())), preferred_element_type=F32)


def normalize(values):
    mean_part = jnp.mean(values, axis=-1, keepdims=True)
    square_part = jnp.mean(values * values, axis=-1, keepdims=True)
    inverse = lax.rsqrt(square_part - mean_part * mean_part + EPS)
    return (values - mean_part) * inverse, inverse


def norm_back(grad_normed, centred, inverse, norm_gain):
    scaled = grad_normed * norm_gain
    first_mean = jnp.mean(scaled, axis=-1, keepdims=True)
    second_mean = jnp.mean(scaled * centred, axis=-1, keepdims=True)
    return inverse * (scaled - first_mean - centred * second_mean)


def gelu_parts(pre_act):
    cdf_value = 0.5 * (1.0 + lax.erf(pre_act * 0.7071067811865476))
    density = jnp.exp(-0.5 * pre_act * pre_act) * 0.3989422804014327
    return (pre_act * cdf_value, cdf_value + pre_act * density)


def columns_sum(values):
    return jnp.sum(values, axis=0, keepdims=True)


def low_lanes(shape):
    return lax.broadcasted_iota(jnp.int32, shape, len(shape) - 1) % LANES < HD


def low(values):
    return jnp.where(low_lanes(values.shape), values, jnp.zeros_like(values))


def high(values):
    return jnp.where(low_lanes(values.shape), jnp.zeros_like(values), values)


def piece_rows(ids, which, size):
    side = ids[1] if which % 2 == 0 else 1 - ids[1]
    return pl.ds(pl.multiple_of((ids[0] ^ (BASES[which // 2] + side)) * size, size), size)


def copies(ids, pieces, full, sems, column=0):
    columns = pl.ds(column, full.shape[1])
    return [
        pltpu.make_async_copy(piece.at[:, columns], full.at[piece_rows(ids, i, piece.shape[0])], sems.at[i])
        for i, piece in enumerate(pieces)
    ]


def place(ids, pieces, full, sems, column=0):
    for copy in copies(ids, pieces, full, sems, column):
        copy.start()
    for copy in copies(ids, pieces, full, sems, column):
        copy.wait()


def place_proj(full, proj):
    one, two, three = (full[:, i * LANES : (i + 1) * LANES].astype(F32) for i in (1, 3, 5))
    proj[:, :LANES] = jnp.where(low_lanes(one.shape), pltpu.roll(one, HD, 1), two).astype(BF)
    proj[:, LANES:] = low(pltpu.roll(three, HD, 1)).astype(BF)


def split_halves(ids, values, mine, away):
    half = values.shape[1] // 2
    left, right = values[:, :half], values[:, half:]
    first = ids[0] % 2 == 0
    mine[...] = jnp.where(first, left, right)
    away[...] = jnp.where(first, right, left)


def join_halves(ids, mine, other):
    first = ids[0] % 2 == 0
    a, b = mine[...].astype(F32), other[...].astype(F32)
    return jnp.concatenate([jnp.where(first, a, b), jnp.where(first, b, a)], axis=1)


def close_kernel(ids, one, two, query, key, value, proj, query_bias, value_bias, proj_bias, gain, shift, hidden_bias, last_bias):
    total = one[...].astype(F32) + two[...].astype(F32)
    size, wide = query.shape
    step = wide + HD
    for i, ref in enumerate((query, key, value)):
        ref[...] = total[:size, i * step : i * step + wide]
    proj[...] = jnp.concatenate([total[:size, i * step + wide : (i + 1) * step] for i in range(3)], axis=1).T
    sums = total[size:]
    gain[...], shift[...], hidden_bias[...] = sums[0], sums[1], sums[4]
    query_bias[...], value_bias[...] = sums[3, :wide], sums[3, 2 * step : 2 * step + wide]
    for ref, row in ((proj_bias, sums[2:3]), (last_bias, sums[5:6])):
        mine = row[:, :wide]
        for i in range(1, row.shape[1] // wide):
            mine = jnp.where(ids[0] == i, row[:, i * wide : (i + 1) * wide], mine)
        ref[...] = mine[0]


def enter_kernel(tokens, cot, gain, shift, tokens_out, first_out, cot_out, sums):
    images = tokens.shape[0] // SEQ
    total = jnp.zeros((1, tokens.shape[1]), F32)
    for i in range(images):
        blank = jnp.zeros((PAD - SEQ, tokens.shape[1]), F32)
        here = pl.ds(i * PAD, PAD)
        rows = jnp.concatenate([tokens[pl.ds(i * SEQ, SEQ), :].astype(F32), blank], axis=0)
        tokens_out[here, :] = rows.astype(BF)
        centred, _ = normalize(rows)
        first_out[here, :] = (centred * gain[...] + shift[...]).astype(BF)
        rows = jnp.concatenate([cot[pl.ds(i * SEQ, SEQ), :].astype(F32), blank], axis=0)
        cot_out[here, :] = rows.astype(BF)
        total += columns_sum(rows)
    sums[...] = total


def attend_kernel(ids, first, h0, h1, h2, h3, bias, proj_bias, joined, attended, probs, mine, away, full, proj, sems):
    @pl.when(pl.program_id(0) == 0)
    def _():
        place(ids, (h0, h1, h2, h3), full, sems)
        place_proj(full, proj)

    rows = (dot(first[...], full[...], (1, 0)) + bias[...]).astype(BF)
    query = rows[:, : 2 * LANES] * jnp.asarray(HD**-0.5, BF)
    joined[:, : 2 * LANES] = query
    joined[:, 2 * LANES :] = rows[:, 2 * LANES :]
    key, value = rows[:, 2 * LANES : 4 * LANES], rows[:, 4 * LANES :]
    is_key = lax.broadcasted_iota(jnp.int32, (PAD, PAD), 1) < SEQ
    outs = []
    for head in range(3):
        lanes = slice(head // 2 * LANES, (head // 2 + 1) * LANES)
        part = high if head == 1 else low
        scores = dot(query[:, lanes], part(key[:, lanes]), (1, 1))
        scores = jnp.where(is_key, scores, -1e30)
        weights = jnp.exp(scores - jnp.max(scores, axis=-1, keepdims=True))
        weights = (weights * (1.0 / jnp.sum(weights, axis=-1, keepdims=True))).astype(BF)
        probs[head] = weights
        outs.append(dot(weights, part(value[:, lanes]), (1, 0)))
    result = jnp.concatenate([outs[0] + outs[1], outs[2]], axis=1).astype(BF)
    attended[...] = result
    split_halves(ids, (dot(result, proj[...], (1, 1)) + proj_bias[...]).astype(BF), mine, away)


def mlp_kernel(
    ids, tokens, one, two, cot, gain, shift, bias, w0, w1, w2, w3,
    second_out, hidden_out, pre_out, mine, away, sums, full, sems
):
    @pl.when(pl.program_id(0) == 0)
    def _():
        for copy in copies(ids, (w0, w1, w2, w3), full, sems):
            copy.start()
        sums[...] = jnp.zeros_like(sums)

    mid = tokens[...].astype(F32) + join_halves(ids, one, two)
    centred, _ = normalize(mid)
    second = (centred * gain[...] + shift[...]).astype(BF)
    second_out[...] = second

    @pl.when(pl.program_id(0) == 0)
    def _():
        for copy in copies(ids, (w0, w1, w2, w3), full, sems):
            copy.wait()

    width = hidden_out.shape[1]
    activ, slope = gelu_parts(dot(second, full[:, :width], (1, 0)) + bias[...])
    hidden_out[...] = activ.astype(BF)
    grad_pre = dot(cot[...], full[:, width:], (1, 0)) * slope
    sums[...] += columns_sum(grad_pre)
    grad_pre = grad_pre.astype(BF)
    pre_out[...] = grad_pre
    split_halves(ids, dot(grad_pre, full[:, :width], (1, 1)).astype(BF), mine, away)


def shrink_kernel(ids, hidden, w0, w1, w2, w3, bias, mine, away, shrink, sems):
    @pl.when(pl.program_id(0) == 0)
    def _():
        place(ids, (w0, w1, w2, w3), shrink, sems, hidden.shape[1])

    split_halves(ids, (dot(hidden[...], shrink[...], (1, 1)) + bias[...]).astype(BF), mine, away)


def deal(ids, full, stay_one, stay_two, away_one, away_two):
    size = stay_one.shape[0]
    for i, ref in enumerate((stay_one, away_one, stay_two, away_two)):
        ref[...] = full[piece_rows(ids, i, size), :].astype(BF)


def outer_kernel(ids, cot, hidden, second, grad_pre, s0, s1, a0, a1, full):
    width = hidden.shape[1]
    full[:, :width] = dot(second[...], grad_pre[...], (0, 0)).astype(BF)
    full[:, width:] = dot(cot[...], hidden[...], (0, 0)).astype(BF)
    deal(ids, full, s0, s1, a0, a1)


def joined_outer_kernel(ids, first, joined, grad_mid, attended, sums, pre_sum, cot_sum, s0, s1, away, full):
    full[...] = dot(first[...], joined[...], (0, 0)).astype(BF)
    other = dot(grad_mid[...], attended[...], (0, 0))
    turned = (pltpu.roll(other[:, :LANES], HD, 1), other[:, :LANES], pltpu.roll(other[:, LANES:], HD, 1))
    for i, values in enumerate(turned):
        lanes = pl.ds((2 * i + 1) * LANES, LANES)
        is_low = low_lanes(values.shape)
        full[:, lanes] = jnp.where(is_low, full[:, lanes].astype(F32), values).astype(BF)
    size = s0.shape[0] - SUMS
    blank = jnp.zeros((SUMS - 6, full.shape[1]), F32)
    below = jnp.concatenate([sums[...], pre_sum[...], cot_sum[...], blank], axis=0).astype(BF)
    places = (s0, s1, away.at[pl.ds(0, size + SUMS)], away.at[pl.ds(size + SUMS, size + SUMS)])
    deal(ids, full, *(ref.at[pl.ds(0, size)] for ref in places))
    for ref in places:
        ref[pl.ds(size, SUMS), :] = below


def attend_back_kernel(
    ids, one, two, tokens, mid_one, mid_two, cot, gain, h0, h1, h2, h3, joined, probs,
    grad_mid_out, grad_joined_out, mine, away, sums, full, proj, sems
):
    @pl.when(pl.program_id(0) == 0)
    def _():
        for copy in copies(ids, (h0, h1, h2, h3), full, sems):
            copy.start()
        sums[...] = jnp.zeros_like(sums)

    grad_normed = join_halves(ids, one, two)
    centred, inverse = normalize(tokens[...].astype(F32) + join_halves(ids, mid_one, mid_two))
    grad_mid = cot[...].astype(F32) + norm_back(grad_normed, centred, inverse, gain[...])
    grad_mid_b = grad_mid.astype(BF)
    grad_mid_out[...] = grad_mid_b

    @pl.when(pl.program_id(0) == 0)
    def _():
        for copy in copies(ids, (h0, h1, h2, h3), full, sems):
            copy.wait()
        place_proj(full, proj)

    grad_att = dot(grad_mid_b, proj[...], (1, 0)).astype(BF)
    query, key, value = (joined[:, i * 2 * LANES : (i + 1) * 2 * LANES] for i in range(3))
    queries, keys, values = [], [], []
    for head in range(3):
        lanes = slice(head // 2 * LANES, (head // 2 + 1) * LANES)
        part = high if head == 1 else low
        weights = probs[head]
        wide = weights.astype(F32)
        grad_weights = dot(grad_att[:, lanes], part(value[:, lanes]), (1, 1))
        row_delta = jnp.sum(wide * grad_weights, axis=-1, keepdims=True)
        grad_scores = (wide * (grad_weights - row_delta)).astype(BF)
        queries.append(dot(grad_scores, part(key[:, lanes]), (1, 0)))
        keys.append(dot(grad_scores, part(query[:, lanes]), (0, 0)))
        values.append(dot(weights, part(grad_att[:, lanes]), (0, 0)))
    scale = HD**-0.5
    result = jnp.concatenate(
        [(queries[0] + queries[1]) * scale, queries[2] * scale, keys[0] + keys[1], keys[2], values[0] + values[1], values[2]],
        axis=1,
    )
    for i, terms in enumerate((grad_normed * centred, grad_normed, grad_mid, result)):
        sums[i : i + 1, :] += columns_sum(terms)
    result = result.astype(BF)
    grad_joined_out[...] = result
    split_halves(ids, dot(result, full[...], (1, 1)).astype(BF), mine, away)


def leave(values, out):
    images = values.shape[0] // PAD
    out[...] = jnp.concatenate([values[i * PAD : i * PAD + SEQ] for i in range(images)], axis=0).astype(out.dtype)


def output_kernel(ids, one, two, tokens, mid_one, mid_two, out):
    mid = tokens[...].astype(F32) + join_halves(ids, mid_one, mid_two)
    leave(mid + join_halves(ids, one, two), out)


def exit_kernel(ids, one, upper, lower, grad_mid, tokens, gain, out, sums):
    two = jnp.concatenate([upper[...].astype(F32), lower[...].astype(F32)], axis=0)
    grad_normed = join_halves(ids, one, two)
    centred, inverse = normalize(tokens[...].astype(F32))
    leave(grad_mid[...].astype(F32) + norm_back(grad_normed, centred, inverse, gain[...]), out)
    sums[...] = jnp.concatenate([columns_sum(grad_normed * centred), columns_sum(grad_normed)], axis=0)


def run(kernel, ids, args, outs, flops, images=None, scratch=()):
    def spec(shape, how):
        if how == 3:
            return pl.BlockSpec(memory_space=pltpu.SMEM)
        if how == 2:
            return pl.BlockSpec(memory_space=pl.ANY)
        if images is None:
            return pl.BlockSpec(memory_space=pltpu.VMEM)
        if how == 0:
            return pl.BlockSpec(shape, lambda i: (0,) * len(shape))
        return pl.BlockSpec((shape[0] // images, *shape[1:]), lambda i: (i,) + (0,) * (len(shape) - 1))

    in_specs = [spec(a.shape, how) for a, how in args]
    arrays = [a for a, _ in args]
    if ids is not None:
        in_specs = [pl.BlockSpec(memory_space=pltpu.SMEM)] + in_specs
        arrays = [ids] + arrays
    size = sum(a.size * a.dtype.itemsize for a in arrays)
    shapes = [jax.ShapeDtypeStruct(*s) for s, _ in outs]
    size += sum(s.size * s.dtype.itemsize for s in shapes)
    how = {} if images is None else {"grid": (images,)}
    return list(pl.pallas_call(
        kernel,
        out_shape=shapes,
        in_specs=in_specs,
        out_specs=[spec(s[0], how) for s, how in outs],
        scratch_shapes=list(scratch),
        compiler_params=pltpu.CompilerParams(vmem_limit_bytes=52 * 1024 * 1024),
        cost_estimate=pl.CostEstimate(flops=1, bytes_accessed=1, transcendentals=0),
        **how,
    )(*arrays))


def on_device(
    tokens,
    attn_gain,
    attn_shift,
    query_weight,
    key_weight,
    value_weight,
    query_bias,
    value_bias,
    proj_weight,
    proj_bias,
    mlp_gain,
    mlp_shift,
    expand_weight,
    expand_bias,
    shrink_weight,
    shrink_bias,
    cotangent,
):
    grid = Grid()
    ids = grid.ids
    wide = query_weight.shape[1]
    model = tokens.shape[1]
    hidden_here = expand_weight.shape[1]
    images = tokens.shape[0] // SEQ
    rows = images * PAD
    heads = wide // HD
    half = model // 2
    assert heads == 3

    def pack(query, key, value, proj):
        parts = []
        for i, array in enumerate((query, key, value)):
            parts += [array, proj[..., i * HD : (i + 1) * HD]]
        return jnp.concatenate(parts, axis=-1)

    packed = pack(query_weight, key_weight, value_weight, proj_weight.T)
    both = jnp.concatenate([expand_weight, shrink_weight], axis=1)
    biases = grid.fetch_own(jnp.concatenate([query_bias, value_bias, expand_bias]))
    p_pieces = gather_block(grid, packed)
    w_pieces = gather_block(grid, after(both, p_pieces[0], p_pieces[2]))
    q_bias, v_bias, e_bias = biases[:wide], biases[wide : 2 * wide], biases[2 * wide :]
    nothing = jnp.zeros_like(q_bias)
    joined_bias = pack(q_bias, nothing, v_bias, nothing)

    def line(vector):
        return vector.reshape(1, -1)

    def spread(bias):
        own = jnp.arange(model) // bias.shape[0] == grid.col
        return line(jnp.where(own, jnp.tile(bias, grid.cols), 0.0))

    tokens_pad, first_in, cot, cot_sum = run(
        enter_kernel,
        None,
        [(tokens, 0), (cotangent, 0), (line(attn_gain), 0), (line(attn_shift), 0)],
        [(((rows, model), BF), 0), (((rows, model), BF), 0), (((rows, model), BF), 0), (((1, model), F32), 0)],
        rows * model * 20,
    )
    weights_scratch = [pltpu.VMEM((model, model), BF), pltpu.VMEM((model, 2 * LANES), BF)]
    halves = [(((rows, half), BF), 1), (((rows, half), BF), 1)]
    joined, attended, probs, mine, away = run(
        attend_kernel,
        ids,
        [(first_in, 1)] + [(a, 2) for a in p_pieces] + [(line(joined_bias), 0), (spread(proj_bias), 0)],
        [
            (((rows, model), BF), 1),
            (((rows, 2 * LANES), BF), 1),
            (((heads * images, PAD, PAD), BF), 1),
        ]
        + halves,
        2 * rows * model * (model + 2 * wide),
        images,
        weights_scratch + [pltpu.SemaphoreType.DMA((4,))],
    )
    _, one = sum_two(grid, mine, away, (w_pieces[1],))
    two = grid.swap(after(one, w_pieces[3]), "col", 1)
    mid_one, mid_two = one, two
    second_in, hidden, grad_pre, mine, away, mlp_sums = run(
        mlp_kernel,
        ids,
        [(tokens_pad, 1), (one, 1), (two, 1), (cot, 1)]
        + [(line(a), 0) for a in (mlp_gain, mlp_shift, e_bias)]
        + [(a, 2) for a in w_pieces],
        [
            (((rows, model), BF), 1),
            (((rows, hidden_here), BF), 1),
            (((rows, hidden_here), BF), 1),
        ]
        + halves
        + [(((1, hidden_here), F32), 0)],
        2 * rows * model * hidden_here * 3,
        images,
        [pltpu.VMEM((model, 2 * hidden_here), BF), pltpu.SemaphoreType.DMA((4,))],
    )

    def pieces(width, more=0):
        return [(((model // grid.cols + more, width), BF), 0)] * 4

    mine, one = sum_two(grid, mine, away)
    hidden = after(hidden, mine)
    parts = run(
        outer_kernel,
        ids,
        [(cot, 0), (hidden, 0), (second_in, 0), (grad_pre, 0)],
        pieces(2 * hidden_here),
        4 * rows * model * hidden_here,
        scratch=[pltpu.VMEM((model, 2 * hidden_here), BF)],
    )
    got = [grid.swap(a, "dp", 1) for a in parts[2:]]
    mine_out, away_out = run(
        shrink_kernel,
        ids,
        [(after(hidden, parts[0]), 1)] + [(a, 2) for a in w_pieces] + [(spread(shrink_bias), 0)],
        halves,
        2 * rows * model * hidden_here,
        images,
        [pltpu.VMEM((model, hidden_here), BF), pltpu.SemaphoreType.DMA((4,))],
    )
    _, out_one = sum_two(grid, mine_out, away_out)
    one = after(one, away_out)
    two = grid.swap(one, "col", 1)

    taller = model // grid.cols + SUMS
    grad_mid, grad_joined, mine, away, back_sums = run(
        attend_back_kernel,
        ids,
        [(a, 1) for a in (one, two, tokens_pad, mid_one, mid_two, cot)]
        + [(line(mlp_gain), 0)]
        + [(a, 2) for a in p_pieces]
        + [(joined, 1), (probs, 1)],
        [(((rows, model), BF), 1)] * 2 + halves + [(((4, model), F32), 0)],
        2 * rows * model * (model + 2 * wide),
        images,
        weights_scratch + [pltpu.SemaphoreType.DMA((4,))],
    )
    sooner = after(parts[0], grad_joined) + got[0]
    packed_parts = run(
        joined_outer_kernel,
        ids,
        [(first_in, 0), (grad_joined, 0), (grad_mid, 0), (attended, 0)]
        + [(back_sums, 0), (mlp_sums, 0), (cot_sum, 0)],
        pieces(model, SUMS)[:2] + [(((2 * (model // grid.cols + SUMS), model), BF), 0)],
        2 * rows * model * model,
        scratch=[pltpu.VMEM((model, model), BF)],
    )
    packed_got = grid.swap(packed_parts[2], "dp", 1)
    packed_got = packed_got[: model // grid.cols + SUMS], packed_got[model // grid.cols + SUMS :]
    later = after(parts[1], packed_parts[0]) + got[1]
    away = after(away, packed_parts[0], later, out_one)
    sooner, later = grid.give(sooner, BASES[0]), grid.give(later, BASES[1])
    mine, one = sum_two(grid, mine, away)
    (output,) = run(
        output_kernel,
        ids,
        [(after(out_one, mine), 0), (grid.swap(out_one, "col", 1), 0)]
        + [(a, 0) for a in (tokens_pad, mid_one, mid_two)],
        [((tokens.shape, BF), 0)],
        rows * model,
    )
    packed_one = after(packed_parts[0], output, sooner) + packed_got[0]
    packed_two = after(packed_parts[1], packed_one) + packed_got[1]
    packed_given = [grid.give(packed_one, BASES[0]), grid.give(packed_two, BASES[1])]
    total = after(sooner, packed_two, one) + later
    one = after(one, total)
    grad_tokens, late = run(
        exit_kernel,
        ids,
        [(after(one, packed_two), 0)]
        + [(grid.swap(part, "col", 1), 0) for part in (one[:CUT], one[CUT:])]
        + [(grad_mid, 0), (tokens_pad, 0), (line(attn_gain), 0)],
        [((tokens.shape, BF), 0), (((2, model), F32), 0)],
        rows * model * 20,
    )
    own, other = finish(grid, total)
    grad_both = own.astype(F32) + other.astype(F32)
    packed_total = after(packed_given[0], grad_tokens) + packed_given[1]
    own, other = finish(grid, packed_total)
    late = sum_axis(grid, after(late, packed_total), "row", 1)
    late = sum_axis(grid, late, "dp", 1)
    square, line_of = (query_weight.shape, F32), lambda size: (((size,), F32), 0)
    (
        grad_query,
        grad_key,
        grad_value,
        grad_proj,
        grad_query_bias,
        grad_value_bias,
        grad_proj_bias,
        grad_mlp_gain,
        grad_mlp_shift,
        grad_expand_bias,
        grad_shrink_bias,
    ) = run(
        close_kernel,
        ids,
        [(own, 0), (other, 0)],
        [(square, 0)] * 4 + [line_of(wide)] * 3 + [line_of(model)] * 3 + [line_of(wide)],
        1,
    )
    return (
        output,
        grad_tokens,
        late[0],
        late[1],
        grad_query,
        grad_key,
        grad_value,
        grad_query_bias,
        grad_value_bias,
        grad_proj,
        grad_proj_bias,
        grad_mlp_gain,
        grad_mlp_shift,
        grad_both[:, :hidden_here],
        grad_expand_bias,
        grad_both[:, hidden_here:],
        grad_shrink_bias,
    )


def solution(mesh):
    placed = (
        P(("dp", "row"), None),
        P(),
        P(),
        P("col", "row"),
        P("col", "row"),
        P("col", "row"),
        P("row"),
        P("row"),
        P("row", "col"),
        P("col"),
        P(),
        P(),
        P("col", "row"),
        P("row"),
        P("col", "row"),
        P("col"),
        P(("dp", "row"), None),
    )
    return jax.shard_map(
        on_device,
        mesh=mesh,
        in_specs=placed,
        out_specs=(
            P(("dp", "row"), None),
            P(("dp", "row"), None),
            P(),
            P(),
            P("col", "row"),
            P("col", "row"),
            P("col", "row"),
            P("row"),
            P("row"),
            P("row", "col"),
            P("col"),
            P(),
            P(),
            P("col", "row"),
            P("row"),
            P("col", "row"),
            P("col"),
        ),
        check_vma=False,
    )
```
